32 devices in a mesh: ctx: 8 (over z, y), ch: 4 (over x, core).
Axes of the slice: x: 2, y: 2, z: 4, core: 2. Of those that a mesh axis runs over, the one named last changes fastest.
Arguments:
- tokens: bfloat16 [2048, 4096], P('ctx', 'ch'), may hold values from -6 to 6
- in_weight: bfloat16 [3, 4096, 4096], P(None, 'ctx', 'ch'), may hold values from -0.09375 to 0.09375
- short_taps: float32 [3, 3, 4096], P(None, None, 'ch'), may hold values from -4 to 4
- long_filter: float32 [4, 1024, 2048], P('ch', 'ctx'), may hold values from -0.125 to 0.125
- skip_gain: float32 [4, 1024], P('ch', 'ctx'), may hold values from 0.25 to 2
Outputs:
- gated_output: bfloat16 [4096, 2048], P('ch', 'ctx')
The draws below stay inside these ranges and needn't reach their ends.
All inputs are finite; a program needn't handle non-finite values.
Results may differ from the reference program's by a relative error of at most 0.015.
Values may be sent and summed in bfloat16 or wider, within the bound.
A program may use at most 128 MiB of HBM per device.

```python
import math
import jax
import jax.numpy as jnp
from jax import lax

D = 4096
LANE_TOTAL = 4096
SITE_SPAN = 2048
N_CH = 4


def block_levels(own_key, shape, split, least, high):
    factor_of = 1.0
    for dim, blocks in split:
        draws = jax.random.uniform(jax.random.fold_in(jax.random.fold_in(own_key, 6), dim), (blocks,), jnp.float32, least / len(split), high / len(split))
        factor_of = factor_of * jnp.repeat(jnp.exp(draws), shape[dim] // blocks).reshape((-1,) + (1,) * (len(shape) - 1 - dim))
    return factor_of


def bell_draw(rng, shape, width, reach, shards=(), dtype=jnp.bfloat16):
    values = jax.random.normal(rng, shape, jnp.float32) * width
    if len(shards) > 0:
        values = block_levels(rng, shape, shards, -0.22, 0.18) * values
    return jnp.clip(values, min=-reach, max=reach).astype(dtype)


def setup_inputs(seed: int = 0) -> dict:
    key_of = jax.random.split(jax.random.key(seed), 6)
    return {
        "tokens": bell_draw(key_of[0], (SITE_SPAN, D), 1.0, 6.0, ((0, 8), (1, 4))),
        "in_weight": bell_draw(key_of[1], (3, D, LANE_TOTAL), D ** -0.5, 0.09375, ((1, 8), (2, 4))),
        "short_taps": bell_draw(key_of[2], (3, 3, LANE_TOTAL), 0.6, 4.0, ((2, 4),), jnp.float32),
        "long_filter": bell_draw(key_of[3], (N_CH, LANE_TOTAL // N_CH, SITE_SPAN), SITE_SPAN ** -0.5, 0.125, ((0, 4), (1, 8)), jnp.float32),
        "skip_gain": jnp.clip(jnp.exp(math.log(2.0) - 2.0794415 * jax.random.uniform(key_of[4], (N_CH, LANE_TOTAL // N_CH), jnp.float32) ** block_levels(key_of[4], (N_CH, LANE_TOTAL // N_CH), ((0, 4), (1, 8)), -0.2, 0.2)), 0.25, 2.0),
    }


def short_conv(projected_float, short_taps):
    context_extent = projected_float.shape[2]
    padded = jnp.pad(projected_float, ((0, 0), (0, 0), (2, 0)))
    result = jnp.zeros_like(projected_float)
    for offset in range(3):
        result = result + short_taps[:, offset, :][:, :, None] * padded[:, :, 2 - offset:2 - offset + context_extent]
    return result


def reference(tokens, in_weight, short_taps, long_filter, skip_gain):
    projected = jnp.stack([jnp.dot(in_weight[which_panel].T, tokens.T, preferred_element_type=jnp.float32) for which_panel in range(3)]).astype(jnp.bfloat16)
    embedding_result = short_conv(projected.astype(jnp.float32), short_taps)
    gate_wave = (embedding_result[1] * embedding_result[2]).astype(jnp.bfloat16)
    kernel_collection = long_filter.reshape(LANE_TOTAL, SITE_SPAN)
    leftover_lines = skip_gain.reshape(LANE_TOTAL)
    lines_in_tile = min(LANE_TOTAL, 256)

    def causal_smear(tile_fragments):
        gate_wave_lines, kernel_table_lines, leftover_fragment = tile_fragments
        padded_extent = 2 * SITE_SPAN
        gate_wave_wide = gate_wave_lines.astype(jnp.float32)
        fourier_coefficients = jnp.fft.rfft(gate_wave_wide, n=padded_extent) * jnp.fft.rfft(kernel_table_lines, n=padded_extent)
        affine_mapping = jnp.fft.irfft(fourier_coefficients, n=padded_extent)[:, :SITE_SPAN]
        return (affine_mapping + leftover_fragment[:, None] * gate_wave_wide).astype(jnp.bfloat16)

    blended_lines = lax.map(causal_smear, (gate_wave.reshape(LANE_TOTAL // lines_in_tile, lines_in_tile, SITE_SPAN), kernel_collection.reshape(LANE_TOTAL // lines_in_tile, lines_in_tile, SITE_SPAN), leftover_lines.reshape(LANE_TOTAL // lines_in_tile, lines_in_tile))).reshape(LANE_TOTAL, SITE_SPAN)
    gated_output = (embedding_result[0] * blended_lines.astype(jnp.float32)).astype(jnp.bfloat16)
    return gated_output
```

```python
import math

import jax
import jax.numpy as jnp
import ml_dtypes
import numpy as np
from jax import lax
from jax.experimental import pallas as pl
from jax.experimental.pallas import tpu as pltpu
from jax.sharding import PartitionSpec as P

BLOCK = 1024


def shifted(block, axis, distance):
    devices = range(lax.axis_size(axis))
    route = [(i - distance, i) for i in devices if i - distance in devices]
    return lax.ppermute(block, axis, route)


def spectral_tables(tile_extent):
    period = 2 * tile_extent
    rows_in = jnp.arange(tile_extent, dtype=jnp.int32)[:, None]
    freq_index = jnp.arange(tile_extent, dtype=jnp.int32)
    first_slot = freq_index == 0
    phases = 2.0 * math.pi / period * (rows_in * freq_index[None, :] % period).astype(jnp.float32)
    top_phase = 2.0 * math.pi / period * (rows_in * tile_extent % period).astype(jnp.float32)
    forward_cos = jnp.cos(phases)
    forward_sin = jnp.where(first_slot[None, :], jnp.cos(top_phase), -jnp.sin(phases))
    times_out = jnp.arange(period, dtype=jnp.int32)[None, :]
    back_phases = (
        2.0 * math.pi / period * (freq_index[:, None] * times_out % period).astype(jnp.float32)
    )
    top_back = 2.0 * math.pi / period * (times_out * tile_extent % period).astype(jnp.float32)
    weights = jnp.where(first_slot, jnp.float32(1.0), jnp.float32(2.0)) / period
    inverse_cos = weights[:, None] * jnp.cos(back_phases)
    inverse_sin = jnp.where(
        first_slot[:, None], jnp.cos(top_back) / period, -(2.0 / period) * jnp.sin(back_phases)
    )
    return (forward_cos, forward_sin, inverse_cos, inverse_sin)


def global_causal_smear(gate_wave, kernel_table_lines, leftover_lines, tile_extent):
    lane_total, context_extent = gate_wave.shape
    tile_sequence_group = context_extent // tile_extent
    forward_cos, forward_sin, inverse_cos, inverse_sin = spectral_tables(tile_extent)
    first_slot = (jnp.arange(tile_extent, dtype=jnp.int32) == 0)[None, None, :]
    highest = lax.Precision.HIGHEST
    gate_wave_wide = gate_wave.astype(jnp.float32)
    source_wave = gate_wave_wide.reshape(lane_total, tile_sequence_group, tile_extent)
    kernel = kernel_table_lines.reshape(lane_total, tile_sequence_group, tile_extent)
    signal_real = jnp.einsum("cnb,bf->cnf", source_wave, forward_cos, precision=highest)
    signal_imag = jnp.einsum("cnb,bf->cnf", source_wave, forward_sin, precision=highest)
    kernel_real = jnp.einsum("cnb,bf->cnf", kernel, forward_cos, precision=highest)
    kernel_imag = jnp.einsum("cnb,bf->cnf", kernel, forward_sin, precision=highest)
    zeros_pad = jnp.zeros((lane_total, tile_sequence_group, tile_extent), jnp.float32)
    padded_real = jnp.concatenate([zeros_pad, signal_real], axis=1)
    padded_imag = jnp.concatenate([zeros_pad, signal_imag], axis=1)

    def accumulate(offset, totals):
        total_real, total_imag = totals
        shifted_real = lax.dynamic_slice_in_dim(
            padded_real, tile_sequence_group - offset, tile_sequence_group, 1
        )
        shifted_imag = lax.dynamic_slice_in_dim(
            padded_imag, tile_sequence_group - offset, tile_sequence_group, 1
        )
        filter_real = lax.dynamic_slice_in_dim(kernel_real, offset, 1, 1)
        filter_imag = lax.dynamic_slice_in_dim(kernel_imag, offset, 1, 1)
        cross = filter_imag * shifted_imag
        next_real = (
            total_real + filter_real * shifted_real - jnp.where(first_slot, jnp.float32(0.0), cross)
        )
        next_imag = total_imag + jnp.where(
            first_slot, cross, filter_real * shifted_imag + filter_imag * shifted_real
        )
        return (next_real, next_imag)

    total_real, total_imag = lax.fori_loop(
        0, tile_sequence_group, accumulate, (zeros_pad, zeros_pad)
    )
    inverse_rows = jnp.einsum("cnf,ft->cnt", total_real, inverse_cos, precision=highest)
    inverse_rows = inverse_rows + jnp.einsum(
        "cnf,ft->cnt", total_imag, inverse_sin, precision=highest
    )
    front_half = inverse_rows[:, :, :tile_extent]
    back_half = inverse_rows[:, :, tile_extent:]
    carried = jnp.concatenate(
        [jnp.zeros((lane_total, 1, tile_extent), jnp.float32), back_half[:, :-1]], axis=1
    )
    affine_mapping = (front_half + carried).reshape(lane_total, context_extent)
    return (affine_mapping + leftover_lines[:, None] * gate_wave_wide).astype(jnp.bfloat16)


def short_conv(projected_float, local_taps, previous):
    context_extent = projected_float.shape[2]
    extended = jnp.concatenate([previous, projected_float], axis=2)
    result = jnp.zeros_like(projected_float)
    for offset in range(3):
        result = (
            result
            + local_taps[:, offset, :][:, :, None]
            * extended[:, :, 2 - offset : 2 - offset + context_extent]
        )
    return result


def shards(tokens, in_weight, short_taps, long_filter, skip_gain):
    whole_tokens = lax.all_gather(tokens, "ch", axis=1, tiled=True)
    local_tokens = whole_tokens.shape[0]
    summed = jnp.einsum(
        "pdc,ld->pcl",
        lax.all_gather(in_weight, "ctx", axis=1, tiled=True),
        whole_tokens,
        preferred_element_type=jnp.float32,
    )
    projected = summed.astype(jnp.bfloat16)
    kernel_table_lines = long_filter[0]
    leftover_lines = skip_gain[0]
    last_rows = projected[:, :, local_tokens - 2 :]
    previous = shifted(last_rows, "ctx", 1)
    embedding_result = short_conv(
        projected.astype(jnp.float32), short_taps, previous.astype(jnp.float32)
    )
    gate_wave = (embedding_result[1] * embedding_result[2]).astype(jnp.bfloat16)
    per_channel_view = lax.all_to_all(gate_wave, "ctx", split_axis=0, concat_axis=1, tiled=True)
    blended_lines = global_causal_smear(per_channel_view, kernel_table_lines, leftover_lines, BLOCK)
    by_token = lax.all_to_all(blended_lines, "ctx", split_axis=1, concat_axis=0, tiled=True)
    gated_output = (embedding_result[0] * by_token.astype(jnp.float32)).astype(jnp.bfloat16)
    return gated_output


NZ, NY, NX, NC = 4, 2, 2, 2
SPECTRAL = 512
MESH_ID = pl.DeviceIdType.MESH


def odd_frequency_tables(tile):
    odd = 2 * np.arange(tile, dtype=np.int64) + 1
    turns = 2.0 * np.pi / (4 * tile)
    times = np.arange(-tile, tile, dtype=np.int64)
    phase = turns * ((odd[:, None] * times[None, :]) % (4 * tile))
    forward = np.concatenate([np.cos(phase), -np.sin(phase)], axis=0)
    back = turns * ((np.arange(tile, dtype=np.int64)[:, None] * odd[None, :]) % (4 * tile))
    inverse = np.concatenate([np.cos(back), -np.sin(back)], axis=1) / tile
    return forward.astype(ml_dtypes.bfloat16), inverse.astype(ml_dtypes.bfloat16)


def mixer_kernel(
    tokens, weight, taps, filters, skip, forward, inverse, out,
    tok, wbuf, proj, spectrum, wave, signal, product, gate, outgoing,
    local_sem, tok_recv, z_send, y_send, x_send, c_send, w_recv, w_send, o_recv, o_send,
):
    ctx_n = NZ * NY
    rows, depth = tokens.shape
    w_depth = weight.shape[1]
    own = filters.shape[1]
    tile = SPECTRAL
    blocks = rows * ctx_n // tile
    i, j = lax.axis_index("ctx"), lax.axis_index("ch")
    z, y = i // NY, i % NY
    x, c = j // NC, j % NC
    low = z // 2

    def device(zz, yy, xx, cc):
        return (zz * NY + yy, xx * NC + cc)

    def block(zz, yy, xx, cc):
        return (zz * NY + yy) * (NX * NC) + xx * NC + cc

    def push(b, sem, target):
        return pltpu.make_async_remote_copy(
            src_ref=tok.at[b], dst_ref=tok.at[b], send_sem=sem, recv_sem=tok_recv.at[b],
            device_id=target, device_id_type=MESH_ID,
        )

    def up(o):
        return push(block(o, y, x, c), z_send.at[o], device(z + 1, y, x, c))

    def down(o):
        return push(block(o, y, x, c), z_send.at[NZ + o], device(z - 1, y, x, c))

    def to_y(o):
        return push(block(o, y, x, c), y_send.at[o], device(z, 1 - y, x, c))

    def to_x(o, yy):
        return push(block(o, yy, x, c), x_send.at[o * NY + yy], device(z, y, 1 - x, c))

    def to_c(o, yy, xx):
        return push(
            block(o, yy, xx, c), c_send.at[(o * NY + yy) * NX + xx], device(z, y, x, 1 - c)
        )

    def arrived(b):
        pltpu.make_async_copy(tok.at[b], tok.at[b], tok_recv.at[b]).wait()

    def rank(r):
        g = r // 2
        return (1 - g) * (z + r * (1 - 2 * (z % 2))) + g * (r + low * (3 - 2 * r))

    barrier = pltpu.get_barrier_semaphore()
    for k in range(1, ctx_n):
        pl.semaphore_signal(
            barrier, inc=1, device_id=((i + k) % ctx_n, j), device_id_type=MESH_ID
        )
    for target in (device(z, y, 1 - x, c), device(z, y, x, 1 - c)):
        pl.semaphore_signal(barrier, inc=1, device_id=target, device_id_type=MESH_ID)
    mine = block(z, y, x, c)
    first = pltpu.make_async_copy(tokens, tok.at[mine], local_sem.at[0])
    first.start()
    own_row = pl.multiple_of(i * w_depth, w_depth)
    own_lane = pl.multiple_of(i * own, own)
    for p in range(3):
        pltpu.make_async_copy(
            weight.at[p, :, pl.ds(own_lane, own)],
            wbuf.at[pl.ds(own_row, w_depth), pl.ds(p * own, own)],
            local_sem.at[1],
        ).start()
    first.wait()
    pl.semaphore_wait(barrier, ctx_n + 1)

    @pl.when(z < NZ - 1)
    def _():
        up(z).start()

    @pl.when(z > 0)
    def _():
        down(z).start()

    to_y(z).start()
    to_x(z, y).start()
    to_c(z, y, x).start()

    def weight_push(k, p):
        peer = (i + k) % ctx_n
        return pltpu.make_async_remote_copy(
            src_ref=weight.at[p, :, pl.ds(pl.multiple_of(peer * own, own), own)],
            dst_ref=wbuf.at[pl.ds(own_row, w_depth), pl.ds(p * own, own)],
            send_sem=w_send.at[(k - 1) * 3 + p], recv_sem=w_recv.at[i],
            device_id=(peer, j), device_id_type=MESH_ID,
        )

    for k in range(1, ctx_n):
        for p in range(3):
            weight_push(k, p).start()

    def z_step(r):
        o = rank(r)
        arrived(block(o, y, x, c))

        @pl.when(jnp.logical_and(o < z, z < NZ - 1))
        def _():
            up(o).start()

        @pl.when(jnp.logical_and(o > z, z > 0))
        def _():
            down(o).start()

        to_y(o).start()
        to_x(o, y).start()
        to_c(o, y, x).start()

    def y_step(r):
        o = rank(r)
        arrived(block(o, 1 - y, x, c))
        to_x(o, 1 - y).start()
        to_c(o, 1 - y, x).start()

    for n in range(blocks):
        lo = max(n - 1, 0) * tile
        window = filters[0, :, lo : (n + 1) * tile].astype(jnp.bfloat16)
        table = forward[:, tile:] if n == 0 else forward[...]
        spectrum[:, n * own : (n + 1) * own] = lax.dot_general(
            table, window, (((1,), (1,)), ((), ())), preferred_element_type=jnp.float32
        )

    z_step(1)
    y_step(0)
    z_step(2)
    y_step(1)
    z_step(3)
    y_step(2)
    y_step(3)

    proj[0:8, :] = jnp.zeros((8, 3 * own), jnp.float32)

    def project(s):
        o, yy = rank(s // 2), (y + s) % 2
        arrived(block(o, yy, x, 1 - c))
        arrived(block(o, yy, 1 - x, 1 - c))
        total = None
        for q in range(NX * NC):
            part = jnp.dot(
                tok[(o * NY + yy) * (NX * NC) + q],
                wbuf[q * depth : (q + 1) * depth, :],
                preferred_element_type=jnp.float32,
            )
            total = part if total is None else total + part
        row = pl.multiple_of(8 + (o * NY + yy) * rows, 8)
        proj[pl.ds(row, rows), :] = total.astype(jnp.bfloat16).astype(jnp.float32)

    def x_step(s):
        o, yy = rank(s // 2), (y + s) % 2
        arrived(block(o, yy, 1 - x, c))
        to_c(o, yy, 1 - x).start()

    lead = 4
    for s in range(lead):
        x_step(s)
    whole_row = wbuf.at[pl.ds(own_row, w_depth), :]
    pltpu.make_async_copy(whole_row, whole_row, local_sem.at[1]).wait()
    for k in range(1, ctx_n):
        peer = (i + k) % ctx_n
        piece = wbuf.at[pl.ds(pl.multiple_of(peer * w_depth, w_depth), w_depth), :]
        pltpu.make_async_copy(piece, piece, w_recv.at[peer]).wait()

    @pl.loop(0, NZ * NY)
    def _(s):
        @pl.when(s < NZ * NY - lead)
        def _():
            x_step(s + lead)

        project(s)

    tap = [
        [taps[p, t : t + 1, pl.ds(own_lane, own)] for t in range(3)] for p in range(3)
    ]
    for q in range(ctx_n):
        start = 8 + q * rows
        feature = []
        for p in range(3):
            lanes = slice(p * own, (p + 1) * own)
            total = tap[p][0] * proj[start : start + rows, lanes]
            total = total + tap[p][1] * proj[start - 1 : start - 1 + rows, lanes]
            feature.append(total + tap[p][2] * proj[start - 2 : start - 2 + rows, lanes])
        gate[q * rows : (q + 1) * rows, :] = feature[0]
        n, at = q * rows // tile, q * rows % tile
        wave[at : at + rows, n * own : (n + 1) * own] = (feature[1] * feature[2]).astype(
            jnp.bfloat16
        )
    signal[...] = jnp.dot(forward[:, tile:], wave[...], preferred_element_type=jnp.float32)

    @pl.loop(0, tile // 16)
    def _(step):
        re = pl.ds(pl.multiple_of(step * 16, 16), 16)
        im = pl.ds(pl.multiple_of(tile + step * 16, 16), 16)
        lanes = [pl.ds(n * own, own) for n in range(blocks)]
        kr, ki = [spectrum[re, a] for a in lanes], [spectrum[im, a] for a in lanes]
        sr, si = [signal[re, a] for a in lanes], [signal[im, a] for a in lanes]
        for n in range(blocks):
            real, imag = 0.0, 0.0
            for m in range(n + 1):
                real = real + (kr[n - m] * sr[m] - ki[n - m] * si[m])
                imag = imag + (kr[n - m] * si[m] + ki[n - m] * sr[m])
            product[re, lanes[n]] = real.astype(jnp.bfloat16)
            product[im, lanes[n]] = imag.astype(jnp.bfloat16)

    def out_push(q):
        return pltpu.make_async_remote_copy(
            src_ref=outgoing.at[q], dst_ref=out.at[pl.ds(own_lane, own), :],
            send_sem=o_send.at[q], recv_sem=o_recv.at[i],
            device_id=(q, j), device_id_type=MESH_ID,
        )

    def out_keep(q):
        return pltpu.make_async_copy(
            outgoing.at[q], out.at[pl.ds(own_lane, own), :], o_send.at[q]
        )

    gain = skip[...]
    for n in range(blocks):
        lanes = slice(n * own, (n + 1) * own)
        smeared = jnp.dot(inverse[...], product[:, lanes], preferred_element_type=jnp.float32)
        for half in range(tile // rows):
            q = n * (tile // rows) + half
            at = slice(half * rows, (half + 1) * rows)
            mixed = smeared[at] + gain * wave[at, lanes].astype(jnp.float32)
            mixed = mixed.astype(jnp.bfloat16).astype(jnp.float32)
            gated = gate[q * rows : (q + 1) * rows, :] * mixed
            outgoing[q] = gated.T.astype(jnp.bfloat16)

            @pl.when(i != q)
            def _():
                out_push(q).start()

            @pl.when(i == q)
            def _():
                out_keep(q).start()

    for o in range(NZ):
        @pl.when(jnp.logical_and(o <= z, z < NZ - 1))
        def _():
            up(o).wait_send()

        @pl.when(jnp.logical_and(o >= z, z > 0))
        def _():
            down(o).wait_send()

        to_y(o).wait_send()
        for yy in range(NY):
            to_x(o, yy).wait_send()
            for xx in range(NX):
                to_c(o, yy, xx).wait_send()
    for k in range(1, ctx_n):
        for p in range(3):
            weight_push(k, p).wait_send()
    for q in range(ctx_n):
        @pl.when(i != q)
        def _():
            out_push(q).wait_send()
            landed = out.at[pl.ds(q * own, own), :]
            pltpu.make_async_copy(landed, landed, o_recv.at[q]).wait()

        @pl.when(i == q)
        def _():
            out_keep(q).wait()


def fused_shards(tokens, in_weight, short_taps, long_filter, skip_gain):
    rows, depth = tokens.shape
    ctx_n, ch_n = NZ * NY, NX * NC
    own = long_filter.shape[1]
    span = rows * ctx_n
    tile = SPECTRAL
    lanes = span // tile * own
    forward, inverse = odd_frequency_tables(tile)
    vmem = pl.BlockSpec(memory_space=pltpu.VMEM)
    hbm = pl.BlockSpec(memory_space=pl.ANY)
    dma = pltpu.SemaphoreType.DMA
    flops = 2 * span * depth * ch_n * 3 * own
    return pl.pallas_call(
        mixer_kernel,
        out_shape=jax.ShapeDtypeStruct((ctx_n * own, rows), jnp.bfloat16),
        in_specs=[hbm, hbm, vmem, vmem, vmem, vmem, vmem],
        out_specs=hbm,
        scratch_shapes=[
            pltpu.VMEM((ctx_n * ch_n, rows, depth), jnp.bfloat16),
            pltpu.VMEM((depth * ch_n, 3 * own), jnp.bfloat16),
            pltpu.VMEM((8 + span, 3 * own), jnp.float32),
            pltpu.VMEM((2 * tile, lanes), jnp.float32),
            pltpu.VMEM((tile, lanes), jnp.bfloat16),
            pltpu.VMEM((2 * tile, lanes), jnp.float32),
            pltpu.VMEM((2 * tile, lanes), jnp.bfloat16),
            pltpu.VMEM((span, own), jnp.float32),
            pltpu.VMEM((ctx_n, own, rows), jnp.bfloat16),
            dma((2,)),
            dma((ctx_n * ch_n,)),
            dma((2 * NZ,)),
            dma((NZ,)),
            dma((ctx_n,)),
            dma((ctx_n * NX,)),
            dma((ctx_n,)),
            dma((3 * (ctx_n - 1),)),
            dma((ctx_n,)),
            dma((ctx_n,)),
        ],
        compiler_params=pltpu.CompilerParams(
            collective_id=0, has_side_effects=True, vmem_limit_bytes=56 * 1024 * 1024
        ),
        cost_estimate=pl.CostEstimate(
            flops=flops, bytes_accessed=2 * tokens.size * ctx_n * ch_n, transcendentals=0
        ),
        name="mixer",
    )(tokens, in_weight, short_taps, long_filter, skip_gain, jnp.asarray(forward), jnp.asarray(inverse))


def fits(mesh, tokens, in_weight, long_filter):
    span, depth = tokens.shape
    return (
        dict(mesh.shape) == {"ctx": NZ * NY, "ch": NX * NC}
        and span == NZ * NY * 256
        and depth == NX * NC * 1024
        and in_weight.shape[2] == long_filter.shape[0] * long_filter.shape[1]
        and long_filter.shape[1] == NZ * NY * 128
    )


def solution(mesh):
    placed = (
        P("ctx", "ch"),
        P(None, "ctx", "ch"),
        P(None, None, "ch"),
        P("ch", "ctx", None),
        P("ch", "ctx"),
    )

    def run(tokens, in_weight, short_taps, long_filter, skip_gain):
        body = fused_shards if fits(mesh, tokens, in_weight, long_filter) else shards
        return jax.shard_map(
            body, mesh=mesh, in_specs=placed, out_specs=P("ch", "ctx"), check_vma=False
        )(tokens, in_weight, short_taps, long_filter, skip_gain)

    return run
```

```python
import math

import jax
import jax.numpy as jnp
import ml_dtypes
import numpy as np
from jax import lax
from jax.experimental import pallas as pl
from jax.experimental.pallas import tpu as pltpu
from jax.sharding import PartitionSpec as P

BLOCK = 1024


def shifted(block, axis, distance):
    devices = range(lax.axis_size(axis))
    route = [(i - distance, i) for i in devices if i - distance in devices]
    return lax.ppermute(block, axis, route)


def spectral_tables(tile_extent):
    period = 2 * tile_extent
    rows_in = jnp.arange(tile_extent, dtype=jnp.int32)[:, None]
    freq_index = jnp.arange(tile_extent, dtype=jnp.int32)
    first_slot = freq_index == 0
    phases = 2.0 * math.pi / period * (rows_in * freq_index[None, :] % period).astype(jnp.float32)
    top_phase = 2.0 * math.pi / period * (rows_in * tile_extent % period).astype(jnp.float32)
    forward_cos = jnp.cos(phases)
    forward_sin = jnp.where(first_slot[None, :], jnp.cos(top_phase), -jnp.sin(phases))
    times_out = jnp.arange(period, dtype=jnp.int32)[None, :]
    back_phases = (
        2.0 * math.pi / period * (freq_index[:, None] * times_out % period).astype(jnp.float32)
    )
    top_back = 2.0 * math.pi / period * (times_out * tile_extent % period).astype(jnp.float32)
    weights = jnp.where(first_slot, jnp.float32(1.0), jnp.float32(2.0)) / period
    inverse_cos = weights[:, None] * jnp.cos(back_phases)
    inverse_sin = jnp.where(
        first_slot[:, None], jnp.cos(top_back) / period, -(2.0 / period) * jnp.sin(back_phases)
    )
    return (forward_cos, forward_sin, inverse_cos, inverse_sin)


def global_causal_smear(gate_wave, kernel_table_lines, leftover_lines, tile_extent):
    lane_total, context_extent = gate_wave.shape
    tile_sequence_group = context_extent // tile_extent
    forward_cos, forward_sin, inverse_cos, inverse_sin = spectral_tables(tile_extent)
    first_slot = (jnp.arange(tile_extent, dtype=jnp.int32) == 0)[None, None, :]
    highest = lax.Precision.HIGHEST
    gate_wave_wide = gate_wave.astype(jnp.float32)
    source_wave = gate_wave_wide.reshape(lane_total, tile_sequence_group, tile_extent)
    kernel = kernel_table_lines.reshape(lane_total, tile_sequence_group, tile_extent)
    signal_real = jnp.einsum("cnb,bf->cnf", source_wave, forward_cos, precision=highest)
    signal_imag = jnp.einsum("cnb,bf->cnf", source_wave, forward_sin, precision=highest)
    kernel_real = jnp.einsum("cnb,bf->cnf", kernel, forward_cos, precision=highest)
    kernel_imag = jnp.einsum("cnb,bf->cnf", kernel, forward_sin, precision=highest)
    zeros_pad = jnp.zeros((lane_total, tile_sequence_group, tile_extent), jnp.float32)
    padded_real = jnp.concatenate([zeros_pad, signal_real], axis=1)
    padded_imag = jnp.concatenate([zeros_pad, signal_imag], axis=1)

    def accumulate(offset, totals):
        total_real, total_imag = totals
        shifted_real = lax.dynamic_slice_in_dim(
            padded_real, tile_sequence_group - offset, tile_sequence_group, 1
        )
        shifted_imag = lax.dynamic_slice_in_dim(
            padded_imag, tile_sequence_group - offset, tile_sequence_group, 1
        )
        filter_real = lax.dynamic_slice_in_dim(kernel_real, offset, 1, 1)
        filter_imag = lax.dynamic_slice_in_dim(kernel_imag, offset, 1, 1)
        cross = filter_imag * shifted_imag
        next_real = (
            total_real + filter_real * shifted_real - jnp.where(first_slot, jnp.float32(0.0), cross)
        )
        next_imag = total_imag + jnp.where(
            first_slot, cross, filter_real * shifted_imag + filter_imag * shifted_real
        )
        return (next_real, next_imag)

    total_real, total_imag = lax.fori_loop(
        0, tile_sequence_group, accumulate, (zeros_pad, zeros_pad)
    )
    inverse_rows = jnp.einsum("cnf,ft->cnt", total_real, inverse_cos, precision=highest)
    inverse_rows = inverse_rows + jnp.einsum(
        "cnf,ft->cnt", total_imag, inverse_sin, precision=highest
    )
    front_half = inverse_rows[:, :, :tile_extent]
    back_half = inverse_rows[:, :, tile_extent:]
    carried = jnp.concatenate(
        [jnp.zeros((lane_total, 1, tile_extent), jnp.float32), back_half[:, :-1]], axis=1
    )
    affine_mapping = (front_half + carried).reshape(lane_total, context_extent)
    return (affine_mapping + leftover_lines[:, None] * gate_wave_wide).astype(jnp.bfloat16)


def short_conv(projected_float, local_taps, previous):
    context_extent = projected_float.shape[2]
    extended = jnp.concatenate([previous, projected_float], axis=2)
    result = jnp.zeros_like(projected_float)
    for offset in range(3):
        result = (
            result
            + local_taps[:, offset, :][:, :, None]
            * extended[:, :, 2 - offset : 2 - offset + context_extent]
        )
    return result


def shards(tokens, in_weight, short_taps, long_filter, skip_gain):
    whole_tokens = lax.all_gather(tokens, "ch", axis=1, tiled=True)
    local_tokens = whole_tokens.shape[0]
    summed = jnp.einsum(
        "pdc,ld->pcl",
        lax.all_gather(in_weight, "ctx", axis=1, tiled=True),
        whole_tokens,
        preferred_element_type=jnp.float32,
    )
    projected = summed.astype(jnp.bfloat16)
    kernel_table_lines = long_filter[0]
    leftover_lines = skip_gain[0]
    last_rows = projected[:, :, local_tokens - 2 :]
    previous = shifted(last_rows, "ctx", 1)
    embedding_result = short_conv(
        projected.astype(jnp.float32), short_taps, previous.astype(jnp.float32)
    )
    gate_wave = (embedding_result[1] * embedding_result[2]).astype(jnp.bfloat16)
    per_channel_view = lax.all_to_all(gate_wave, "ctx", split_axis=0, concat_axis=1, tiled=True)
    blended_lines = global_causal_smear(per_channel_view, kernel_table_lines, leftover_lines, BLOCK)
    by_token = lax.all_to_all(blended_lines, "ctx", split_axis=1, concat_axis=0, tiled=True)
    gated_output = (embedding_result[0] * by_token.astype(jnp.float32)).astype(jnp.bfloat16)
    return gated_output


NZ, NY, NX, NC = 4, 2, 2, 2
SPECTRAL = 512
MESH_ID = pl.DeviceIdType.MESH


def odd_frequency_tables(tile):
    odd = 2 * np.arange(tile, dtype=np.int64) + 1
    turns = 2.0 * np.pi / (4 * tile)
    times = np.arange(-tile, tile, dtype=np.int64)
    phase = turns * ((odd[:, None] * times[None, :]) % (4 * tile))
    forward = np.concatenate([np.cos(phase), -np.sin(phase)], axis=0)
    back = turns * ((np.arange(tile, dtype=np.int64)[:, None] * odd[None, :]) % (4 * tile))
    inverse = np.concatenate([np.cos(back), -np.sin(back)], axis=1) / tile
    return forward.astype(ml_dtypes.bfloat16), inverse.astype(ml_dtypes.bfloat16)


def mixer_kernel(
    tokens, weight, taps, filters_in, skip, forward_in, inverse_in, out,
    filters, forward, inverse, tok, wbuf, proj, spectrum, wave, signal, product, gate, outgoing,
    local_sem, tok_recv, z_send, y_send, x_send, c_send, w_recv, w_send, o_recv, o_send,
):
    ctx_n = NZ * NY
    rows, depth = tokens.shape
    w_depth = weight.shape[1]
    own = filters.shape[1]
    staged = ((filters_in, filters), (forward_in, forward), (inverse_in, inverse))
    tile = SPECTRAL
    blocks = rows * ctx_n // tile
    i, j = lax.axis_index("ctx"), lax.axis_index("ch")
    z, y = i // NY, i % NY
    x, c = j // NC, j % NC
    low = z // 2

    def device(zz, yy, xx, cc):
        return (zz * NY + yy, xx * NC + cc)

    def block(zz, yy, xx, cc):
        return (zz * NY + yy) * (NX * NC) + xx * NC + cc

    def push(b, sem, target):
        return pltpu.make_async_remote_copy(
            src_ref=tok.at[b], dst_ref=tok.at[b], send_sem=sem, recv_sem=tok_recv.at[b],
            device_id=target, device_id_type=MESH_ID,
        )

    def up(o):
        return push(block(o, y, x, c), z_send.at[o], device(z + 1, y, x, c))

    def down(o):
        return push(block(o, y, x, c), z_send.at[NZ + o], device(z - 1, y, x, c))

    def to_y(o):
        return push(block(o, y, x, c), y_send.at[o], device(z, 1 - y, x, c))

    def to_x(o, yy):
        return push(block(o, yy, x, c), x_send.at[o * NY + yy], device(z, y, 1 - x, c))

    def to_c(o, yy, xx):
        return push(
            block(o, yy, xx, c), c_send.at[(o * NY + yy) * NX + xx], device(z, y, x, 1 - c)
        )

    def arrived(b):
        pltpu.make_async_copy(tok.at[b], tok.at[b], tok_recv.at[b]).wait()

    def rank(r):
        g = r // 2
        return (1 - g) * (z + r * (1 - 2 * (z % 2))) + g * (r + low * (3 - 2 * r))

    barrier = pltpu.get_barrier_semaphore()
    for k in range(1, ctx_n):
        pl.semaphore_signal(
            barrier, inc=1, device_id=((i + k) % ctx_n, j), device_id_type=MESH_ID
        )
    for target in (device(z, y, 1 - x, c), device(z, y, x, 1 - c)):
        pl.semaphore_signal(barrier, inc=1, device_id=target, device_id_type=MESH_ID)
    mine = block(z, y, x, c)
    first = pltpu.make_async_copy(tokens, tok.at[mine], local_sem.at[0])
    first.start()
    own_row = pl.multiple_of(i * w_depth, w_depth)
    own_lane = pl.multiple_of(i * own, own)
    for p in range(3):
        pltpu.make_async_copy(
            weight.at[p, :, pl.ds(own_lane, own)],
            wbuf.at[pl.ds(own_row, w_depth), pl.ds(p * own, own)],
            local_sem.at[1],
        ).start()
    for k, (src, dst) in enumerate(staged):
        pltpu.make_async_copy(src, dst, local_sem.at[2 + k]).start()
    first.wait()
    pl.semaphore_wait(barrier, ctx_n + 1)

    @pl.when(z < NZ - 1)
    def _():
        up(z).start()

    @pl.when(z > 0)
    def _():
        down(z).start()

    to_y(z).start()
    to_x(z, y).start()
    to_c(z, y, x).start()

    def weight_push(peer, p):
        return pltpu.make_async_remote_copy(
            src_ref=weight.at[p, :, pl.ds(pl.multiple_of(peer * own, own), own)],
            dst_ref=wbuf.at[pl.ds(own_row, w_depth), pl.ds(p * own, own)],
            send_sem=w_send.at[peer * 3 + p], recv_sem=w_recv.at[i],
            device_id=(peer, j), device_id_type=MESH_ID,
        )

    def push_weights(zz, ys):
        for yy in ys:
            for p in range(3):
                weight_push(zz * NY + yy, p).start()

    def z_step(r):
        o = rank(r)
        arrived(block(o, y, x, c))

        @pl.when(jnp.logical_and(o < z, z < NZ - 1))
        def _():
            up(o).start()

        @pl.when(jnp.logical_and(o > z, z > 0))
        def _():
            down(o).start()

        to_y(o).start()
        to_x(o, y).start()
        to_c(o, y, x).start()

    def y_step(r):
        o = rank(r)
        arrived(block(o, 1 - y, x, c))
        to_x(o, 1 - y).start()
        to_c(o, 1 - y, x).start()

    for k, (src, dst) in enumerate(staged):
        pltpu.make_async_copy(src, dst, local_sem.at[2 + k]).wait()

    for n in range(blocks):
        lo = max(n - 1, 0) * tile
        window = filters[0, :, lo : (n + 1) * tile].astype(jnp.bfloat16)
        table = forward[:, tile:] if n == 0 else forward[...]
        spectrum[:, n * own : (n + 1) * own] = lax.dot_general(
            table, window, (((1,), (1,)), ((), ())), preferred_element_type=jnp.float32
        )

    z_step(1)
    y_step(0)
    push_weights(z, (1 - y,))
    z_step(2)
    push_weights(rank(3), (y, 1 - y))
    push_weights(rank(2), (y, 1 - y))
    push_weights(rank(1), (y, 1 - y))
    y_step(1)
    z_step(3)
    y_step(2)
    y_step(3)

    proj[0:8, :] = jnp.zeros((8, 3 * own), jnp.float32)

    def project(s, ranks, begin, end):
        o, yy = rank(s // 2), (y + s) % 2
        row = pl.multiple_of(8 + (o * NY + yy) * rows, 8)
        total = None if begin else proj[pl.ds(row, rows), :]
        for r in ranks:
            q = rank(r)
            part = jnp.dot(
                tok[(o * NY + yy) * (NX * NC) + q],
                wbuf[pl.ds(pl.multiple_of(q * depth, depth), depth), :],
                preferred_element_type=jnp.float32,
            )
            total = part if total is None else total + part
        if end:
            total = total.astype(jnp.bfloat16).astype(jnp.float32)
        proj[pl.ds(row, rows), :] = total

    def weights_from(zz, ys):
        for yy in ys:
            peer = zz * NY + yy
            piece = wbuf.at[pl.ds(pl.multiple_of(peer * w_depth, w_depth), w_depth), :]
            pltpu.make_async_copy(piece, piece, w_recv.at[peer]).wait()

    def x_step(s):
        o, yy = rank(s // 2), (y + s) % 2
        arrived(block(o, yy, 1 - x, c))
        to_c(o, yy, 1 - x).start()

    lead = 4
    for s in range(lead):
        x_step(s)
    whole_row = wbuf.at[pl.ds(own_row, w_depth), :]
    pltpu.make_async_copy(whole_row, whole_row, local_sem.at[1]).wait()
    weights_from(z, (1 - y,))
    weights_from(rank(1), (y, 1 - y))

    @pl.loop(0, NZ * NY)
    def _(s):
        @pl.when(s < NZ * NY - lead)
        def _():
            x_step(s + lead)

        o, yy = rank(s // 2), (y + s) % 2
        arrived(block(o, yy, x, 1 - c))
        arrived(block(o, yy, 1 - x, 1 - c))
        project(s, (0, 1), True, False)

    weights_from(rank(2), (y, 1 - y))
    weights_from(rank(3), (y, 1 - y))

    @pl.loop(0, NZ * NY)
    def _(s):
        project(s, (2, 3), False, True)

    tap = [
        [taps[p, t : t + 1, pl.ds(own_lane, own)] for t in range(3)] for p in range(3)
    ]
    for q in range(ctx_n):
        start = 8 + q * rows
        feature = []
        for p in range(3):
            lanes = slice(p * own, (p + 1) * own)
            total = tap[p][0] * proj[start : start + rows, lanes]
            total = total + tap[p][1] * proj[start - 1 : start - 1 + rows, lanes]
            feature.append(total + tap[p][2] * proj[start - 2 : start - 2 + rows, lanes])
        gate[q * rows : (q + 1) * rows, :] = feature[0]
        n, at = q * rows // tile, q * rows % tile
        wave[at : at + rows, n * own : (n + 1) * own] = (feature[1] * feature[2]).astype(
            jnp.bfloat16
        )
    signal[...] = jnp.dot(forward[:, tile:], wave[...], preferred_element_type=jnp.float32)

    @pl.loop(0, tile // 16)
    def _(step):
        re = pl.ds(pl.multiple_of(step * 16, 16), 16)
        im = pl.ds(pl.multiple_of(tile + step * 16, 16), 16)
        lanes = [pl.ds(n * own, own) for n in range(blocks)]
        kr, ki = [spectrum[re, a] for a in lanes], [spectrum[im, a] for a in lanes]
        sr, si = [signal[re, a] for a in lanes], [signal[im, a] for a in lanes]
        for n in range(blocks):
            real, imag = 0.0, 0.0
            for m in range(n + 1):
                real = real + (kr[n - m] * sr[m] - ki[n - m] * si[m])
                imag = imag + (kr[n - m] * si[m] + ki[n - m] * sr[m])
            product[re, lanes[n]] = real.astype(jnp.bfloat16)
            product[im, lanes[n]] = imag.astype(jnp.bfloat16)

    def out_push(q):
        return pltpu.make_async_remote_copy(
            src_ref=outgoing.at[q], dst_ref=out.at[pl.ds(own_lane, own), :],
            send_sem=o_send.at[q], recv_sem=o_recv.at[i],
            device_id=(q, j), device_id_type=MESH_ID,
        )

    def out_keep(q):
        return pltpu.make_async_copy(
            outgoing.at[q], out.at[pl.ds(own_lane, own), :], o_send.at[q]
        )

    gain = skip[...]
    for n in range(blocks):
        lanes = slice(n * own, (n + 1) * own)
        smeared = jnp.dot(inverse[...], product[:, lanes], preferred_element_type=jnp.float32)
        for half in range(tile // rows):
            q = n * (tile // rows) + half
            at = slice(half * rows, (half + 1) * rows)
            mixed = smeared[at] + gain * wave[at, lanes].astype(jnp.float32)
            mixed = mixed.astype(jnp.bfloat16).astype(jnp.float32)
            gated = gate[q * rows : (q + 1) * rows, :] * mixed
            outgoing[q] = gated.T.astype(jnp.bfloat16)

            @pl.when(i != q)
            def _():
                out_push(q).start()

            @pl.when(i == q)
            def _():
                out_keep(q).start()

    for o in range(NZ):
        @pl.when(jnp.logical_and(o <= z, z < NZ - 1))
        def _():
            up(o).wait_send()

        @pl.when(jnp.logical_and(o >= z, z > 0))
        def _():
            down(o).wait_send()

        to_y(o).wait_send()
        for yy in range(NY):
            to_x(o, yy).wait_send()
            for xx in range(NX):
                to_c(o, yy, xx).wait_send()
    for q in range(ctx_n):
        @pl.when(i != q)
        def _():
            for p in range(3):
                weight_push(q, p).wait_send()
            out_push(q).wait_send()
            landed = out.at[pl.ds(q * own, own), :]
            pltpu.make_async_copy(landed, landed, o_recv.at[q]).wait()

        @pl.when(i == q)
        def _():
            out_keep(q).wait()


def fused_shards(tokens, in_weight, short_taps, long_filter, skip_gain):
    rows, depth = tokens.shape
    ctx_n, ch_n = NZ * NY, NX * NC
    own = long_filter.shape[1]
    span = rows * ctx_n
    tile = SPECTRAL
    lanes = span // tile * own
    forward, inverse = odd_frequency_tables(tile)
    vmem = pl.BlockSpec(memory_space=pltpu.VMEM)
    hbm = pl.BlockSpec(memory_space=pl.ANY)
    dma = pltpu.SemaphoreType.DMA
    flops = 2 * span * depth * ch_n * 3 * own
    return pl.pallas_call(
        mixer_kernel,
        out_shape=jax.ShapeDtypeStruct((ctx_n * own, rows), jnp.bfloat16),
        in_specs=[hbm, hbm, vmem, hbm, vmem, hbm, hbm],
        out_specs=hbm,
        scratch_shapes=[
            pltpu.VMEM(long_filter.shape, jnp.float32),
            pltpu.VMEM(forward.shape, jnp.bfloat16),
            pltpu.VMEM(inverse.shape, jnp.bfloat16),
            pltpu.VMEM((ctx_n * ch_n, rows, depth), jnp.bfloat16),
            pltpu.VMEM((depth * ch_n, 3 * own), jnp.bfloat16),
            pltpu.VMEM((8 + span, 3 * own), jnp.float32),
            pltpu.VMEM((2 * tile, lanes), jnp.float32),
            pltpu.VMEM((tile, lanes), jnp.bfloat16),
            pltpu.VMEM((2 * tile, lanes), jnp.float32),
            pltpu.VMEM((2 * tile, lanes), jnp.bfloat16),
            pltpu.VMEM((span, own), jnp.float32),
            pltpu.VMEM((ctx_n, own, rows), jnp.bfloat16),
            dma((5,)),
            dma((ctx_n * ch_n,)),
            dma((2 * NZ,)),
            dma((NZ,)),
            dma((ctx_n,)),
            dma((ctx_n * NX,)),
            dma((ctx_n,)),
            dma((3 * ctx_n,)),
            dma((ctx_n,)),
            dma((ctx_n,)),
        ],
        compiler_params=pltpu.CompilerParams(
            collective_id=0, has_side_effects=True, vmem_limit_bytes=56 * 1024 * 1024
        ),
        cost_estimate=pl.CostEstimate(
            flops=flops, bytes_accessed=2 * tokens.size * ctx_n * ch_n, transcendentals=0
        ),
        name="mixer",
    )(tokens, in_weight, short_taps, long_filter, skip_gain, jnp.asarray(forward), jnp.asarray(inverse))


def fits(mesh, tokens, in_weight, long_filter):
    span, depth = tokens.shape
    return (
        dict(mesh.shape) == {"ctx": NZ * NY, "ch": NX * NC}
        and span == NZ * NY * 256
        and depth == NX * NC * 1024
        and in_weight.shape[2] == long_filter.shape[0] * long_filter.shape[1]
        and long_filter.shape[1] == NZ * NY * 128
    )


def solution(mesh):
    placed = (
        P("ctx", "ch"),
        P(None, "ctx", "ch"),
        P(None, None, "ch"),
        P("ch", "ctx", None),
        P("ch", "ctx"),
    )

    def run(tokens, in_weight, short_taps, long_filter, skip_gain):
        body = fused_shards if fits(mesh, tokens, in_weight, long_filter) else shards
        return jax.shard_map(
            body, mesh=mesh, in_specs=placed, out_specs=P("ch", "ctx"), check_vma=False
        )(tokens, in_weight, short_taps, long_filter, skip_gain)

    return run
```

```python
import math

import jax
import jax.numpy as jnp
import ml_dtypes
import numpy as np
from jax import lax
from jax.experimental import pallas as pl
from jax.experimental.pallas import tpu as pltpu
from jax.sharding import PartitionSpec as P

BLOCK = 1024


def shifted(block, axis, distance):
    devices = range(lax.axis_size(axis))
    route = [(i - distance, i) for i in devices if i - distance in devices]
    return lax.ppermute(block, axis, route)


def spectral_tables(tile_extent):
    period = 2 * tile_extent
    rows_in = jnp.arange(tile_extent, dtype=jnp.int32)[:, None]
    freq_index = jnp.arange(tile_extent, dtype=jnp.int32)
    first_slot = freq_index == 0
    phases = 2.0 * math.pi / period * (rows_in * freq_index[None, :] % period).astype(jnp.float32)
    top_phase = 2.0 * math.pi / period * (rows_in * tile_extent % period).astype(jnp.float32)
    forward_cos = jnp.cos(phases)
    forward_sin = jnp.where(first_slot[None, :], jnp.cos(top_phase), -jnp.sin(phases))
    times_out = jnp.arange(period, dtype=jnp.int32)[None, :]
    back_phases = (
        2.0 * math.pi / period * (freq_index[:, None] * times_out % period).astype(jnp.float32)
    )
    top_back = 2.0 * math.pi / period * (times_out * tile_extent % period).astype(jnp.float32)
    weights = jnp.where(first_slot, jnp.float32(1.0), jnp.float32(2.0)) / period
    inverse_cos = weights[:, None] * jnp.cos(back_phases)
    inverse_sin = jnp.where(
        first_slot[:, None], jnp.cos(top_back) / period, -(2.0 / period) * jnp.sin(back_phases)
    )
    return (forward_cos, forward_sin, inverse_cos, inverse_sin)


def global_causal_smear(gate_wave, kernel_table_lines, leftover_lines, tile_extent):
    lane_total, context_extent = gate_wave.shape
    tile_sequence_group = context_extent // tile_extent
    forward_cos, forward_sin, inverse_cos, inverse_sin = spectral_tables(tile_extent)
    first_slot = (jnp.arange(tile_extent, dtype=jnp.int32) == 0)[None, None, :]
    highest = lax.Precision.HIGHEST
    gate_wave_wide = gate_wave.astype(jnp.float32)
    source_wave = gate_wave_wide.reshape(lane_total, tile_sequence_group, tile_extent)
    kernel = kernel_table_lines.reshape(lane_total, tile_sequence_group, tile_extent)
    signal_real = jnp.einsum("cnb,bf->cnf", source_wave, forward_cos, precision=highest)
    signal_imag = jnp.einsum("cnb,bf->cnf", source_wave, forward_sin, precision=highest)
    kernel_real = jnp.einsum("cnb,bf->cnf", kernel, forward_cos, precision=highest)
    kernel_imag = jnp.einsum("cnb,bf->cnf", kernel, forward_sin, precision=highest)
    zeros_pad = jnp.zeros((lane_total, tile_sequence_group, tile_extent), jnp.float32)
    padded_real = jnp.concatenate([zeros_pad, signal_real], axis=1)
    padded_imag = jnp.concatenate([zeros_pad, signal_imag], axis=1)

    def accumulate(offset, totals):
        total_real, total_imag = totals
        shifted_real = lax.dynamic_slice_in_dim(
            padded_real, tile_sequence_group - offset, tile_sequence_group, 1
        )
        shifted_imag = lax.dynamic_slice_in_dim(
            padded_imag, tile_sequence_group - offset, tile_sequence_group, 1
        )
        filter_real = lax.dynamic_slice_in_dim(kernel_real, offset, 1, 1)
        filter_imag = lax.dynamic_slice_in_dim(kernel_imag, offset, 1, 1)
        cross = filter_imag * shifted_imag
        next_real = (
            total_real + filter_real * shifted_real - jnp.where(first_slot, jnp.float32(0.0), cross)
        )
        next_imag = total_imag + jnp.where(
            first_slot, cross, filter_real * shifted_imag + filter_imag * shifted_real
        )
        return (next_real, next_imag)

    total_real, total_imag = lax.fori_loop(
        0, tile_sequence_group, accumulate, (zeros_pad, zeros_pad)
    )
    inverse_rows = jnp.einsum("cnf,ft->cnt", total_real, inverse_cos, precision=highest)
    inverse_rows = inverse_rows + jnp.einsum(
        "cnf,ft->cnt", total_imag, inverse_sin, precision=highest
    )
    front_half = inverse_rows[:, :, :tile_extent]
    back_half = inverse_rows[:, :, tile_extent:]
    carried = jnp.concatenate(
        [jnp.zeros((lane_total, 1, tile_extent), jnp.float32), back_half[:, :-1]], axis=1
    )
    affine_mapping = (front_half + carried).reshape(lane_total, context_extent)
    return (affine_mapping + leftover_lines[:, None] * gate_wave_wide).astype(jnp.bfloat16)


def short_conv(projected_float, local_taps, previous):
    context_extent = projected_float.shape[2]
    extended = jnp.concatenate([previous, projected_float], axis=2)
    result = jnp.zeros_like(projected_float)
    for offset in range(3):
        result = (
            result
            + local_taps[:, offset, :][:, :, None]
            * extended[:, :, 2 - offset : 2 - offset + context_extent]
        )
    return result


def shards(tokens, in_weight, short_taps, long_filter, skip_gain):
    whole_tokens = lax.all_gather(tokens, "ch", axis=1, tiled=True)
    local_tokens = whole_tokens.shape[0]
    summed = jnp.einsum(
        "pdc,ld->pcl",
        lax.all_gather(in_weight, "ctx", axis=1, tiled=True),
        whole_tokens,
        preferred_element_type=jnp.float32,
    )
    projected = summed.astype(jnp.bfloat16)
    kernel_table_lines = long_filter[0]
    leftover_lines = skip_gain[0]
    last_rows = projected[:, :, local_tokens - 2 :]
    previous = shifted(last_rows, "ctx", 1)
    embedding_result = short_conv(
        projected.astype(jnp.float32), short_taps, previous.astype(jnp.float32)
    )
    gate_wave = (embedding_result[1] * embedding_result[2]).astype(jnp.bfloat16)
    per_channel_view = lax.all_to_all(gate_wave, "ctx", split_axis=0, concat_axis=1, tiled=True)
    blended_lines = global_causal_smear(per_channel_view, kernel_table_lines, leftover_lines, BLOCK)
    by_token = lax.all_to_all(blended_lines, "ctx", split_axis=1, concat_axis=0, tiled=True)
    gated_output = (embedding_result[0] * by_token.astype(jnp.float32)).astype(jnp.bfloat16)
    return gated_output


NZ, NY, NX, NC = 4, 2, 2, 2
SPECTRAL = 512
MESH_ID = pl.DeviceIdType.MESH


def odd_frequency_tables(tile):
    odd = 2 * np.arange(tile, dtype=np.int64) + 1
    turns = 2.0 * np.pi / (4 * tile)
    times = np.arange(-tile, tile, dtype=np.int64)
    phase = turns * ((odd[:, None] * times[None, :]) % (4 * tile))
    forward = np.concatenate([np.cos(phase), -np.sin(phase)], axis=0)
    back = turns * ((np.arange(tile, dtype=np.int64)[:, None] * odd[None, :]) % (4 * tile))
    inverse = np.concatenate([np.cos(back), -np.sin(back)], axis=1) / tile
    return forward.astype(ml_dtypes.bfloat16), inverse.astype(ml_dtypes.bfloat16)


def mixer_kernel(
    tokens, weight, taps, filters_in, skip, forward_in, inverse_in, out,
    filters, forward, inverse, tok, wsend, wbuf, proj, spectrum, wave, signal, product, gate, outgoing,
    local_sem, tok_recv, z_send, y_send, x_send, c_send, w_recv, w_send, o_recv, o_send,
):
    ctx_n = NZ * NY
    rows, depth = tokens.shape
    w_depth = weight.shape[1]
    own = filters.shape[1]
    staged = ((filters_in, filters), (forward_in, forward), (inverse_in, inverse))
    tile = SPECTRAL
    blocks = rows * ctx_n // tile
    i, j = lax.axis_index("ctx"), lax.axis_index("ch")
    z, y = i // NY, i % NY
    x, c = j // NC, j % NC
    low = z // 2

    def device(zz, yy, xx, cc):
        return (zz * NY + yy, xx * NC + cc)

    def block(zz, yy, xx, cc):
        return (zz * NY + yy) * (NX * NC) + xx * NC + cc

    def push(b, sem, target):
        return pltpu.make_async_remote_copy(
            src_ref=tok.at[b], dst_ref=tok.at[b], send_sem=sem, recv_sem=tok_recv.at[b],
            device_id=target, device_id_type=MESH_ID,
        )

    def up(o):
        return push(block(o, y, x, c), z_send.at[o], device(z + 1, y, x, c))

    def down(o):
        return push(block(o, y, x, c), z_send.at[NZ + o], device(z - 1, y, x, c))

    def to_y(o):
        return push(block(o, y, x, c), y_send.at[o], device(z, 1 - y, x, c))

    def to_x(o, yy):
        return push(block(o, yy, x, c), x_send.at[o * NY + yy], device(z, y, 1 - x, c))

    def to_c(o, yy, xx):
        return push(
            block(o, yy, xx, c), c_send.at[(o * NY + yy) * NX + xx], device(z, y, x, 1 - c)
        )

    def arrived(b):
        pltpu.make_async_copy(tok.at[b], tok.at[b], tok_recv.at[b]).wait()

    def rank(r):
        g = r // 2
        return (1 - g) * (z + r * (1 - 2 * (z % 2))) + g * (r + low * (3 - 2 * r))

    barrier = pltpu.get_barrier_semaphore()
    for k in range(1, ctx_n):
        pl.semaphore_signal(
            barrier, inc=1, device_id=((i + k) % ctx_n, j), device_id_type=MESH_ID
        )
    for target in (device(z, y, 1 - x, c), device(z, y, x, 1 - c)):
        pl.semaphore_signal(barrier, inc=1, device_id=target, device_id_type=MESH_ID)
    mine = block(z, y, x, c)
    first = pltpu.make_async_copy(tokens, tok.at[mine], local_sem.at[0])
    first.start()
    own_row = pl.multiple_of(i * w_depth, w_depth)
    own_lane = pl.multiple_of(i * own, own)
    for peer in range(ctx_n):
        for p in range(3):
            pltpu.make_async_copy(
                weight.at[p, :, pl.ds(peer * own, own)],
                wsend.at[peer, :, pl.ds(p * own, own)],
                local_sem.at[1],
            ).start()
    for k, (src, dst) in enumerate(staged):
        pltpu.make_async_copy(src, dst, local_sem.at[2 + k]).start()
    first.wait()
    pl.semaphore_wait(barrier, ctx_n + 1)

    @pl.when(z < NZ - 1)
    def _():
        up(z).start()

    @pl.when(z > 0)
    def _():
        down(z).start()

    to_y(z).start()
    to_x(z, y).start()
    to_c(z, y, x).start()

    def weight_push(peer):
        return pltpu.make_async_remote_copy(
            src_ref=wsend.at[peer], dst_ref=wbuf.at[pl.ds(own_row, w_depth), :],
            send_sem=w_send.at[peer], recv_sem=w_recv.at[i],
            device_id=(peer, j), device_id_type=MESH_ID,
        )

    def push_weights(zz, ys):
        for yy in ys:
            weight_push(zz * NY + yy).start()

    def z_step(r):
        o = rank(r)
        arrived(block(o, y, x, c))

        @pl.when(jnp.logical_and(o < z, z < NZ - 1))
        def _():
            up(o).start()

        @pl.when(jnp.logical_and(o > z, z > 0))
        def _():
            down(o).start()

        to_y(o).start()
        to_x(o, y).start()
        to_c(o, y, x).start()

    def y_step(r):
        o = rank(r)
        arrived(block(o, 1 - y, x, c))
        to_x(o, 1 - y).start()
        to_c(o, 1 - y, x).start()

    for k, (src, dst) in enumerate(staged):
        pltpu.make_async_copy(src, dst, local_sem.at[2 + k]).wait()

    for n in range(blocks):
        lo = max(n - 1, 0) * tile
        window = filters[0, :, lo : (n + 1) * tile].astype(jnp.bfloat16)
        table = forward[:, tile:] if n == 0 else forward[...]
        spectrum[:, n * own : (n + 1) * own] = lax.dot_general(
            table, window, (((1,), (1,)), ((), ())), preferred_element_type=jnp.float32
        )

    pltpu.make_async_copy(wsend, wsend, local_sem.at[1]).wait()
    own_weights = pltpu.make_async_copy(
        wsend.at[i], wbuf.at[pl.ds(own_row, w_depth), :], local_sem.at[5]
    )
    own_weights.start()

    z_step(1)
    y_step(0)
    push_weights(z, (1 - y,))
    z_step(2)
    push_weights(rank(3), (y, 1 - y))
    y_step(1)
    z_step(3)
    push_weights(rank(2), (y, 1 - y))
    y_step(2)
    push_weights(rank(1), (y, 1 - y))
    y_step(3)

    proj[0:8, :] = jnp.zeros((8, 3 * own), jnp.float32)

    def project(at, ranks, begin, end):
        row = 8 + at * rows if isinstance(at, int) else pl.multiple_of(8 + at * rows, 8)
        total = None if begin else proj[pl.ds(row, rows), :]
        for r in ranks:
            q = rank(r)
            part = jnp.dot(
                tok[at * (NX * NC) + q],
                wbuf[pl.ds(pl.multiple_of(q * depth, depth), depth), :],
                preferred_element_type=jnp.float32,
            )
            total = part if total is None else total + part
        if end:
            total = total.astype(jnp.bfloat16).astype(jnp.float32)
        proj[pl.ds(row, rows), :] = total

    def weights_from(zz, ys):
        for yy in ys:
            peer = zz * NY + yy
            piece = wbuf.at[pl.ds(pl.multiple_of(peer * w_depth, w_depth), w_depth), :]
            pltpu.make_async_copy(piece, piece, w_recv.at[peer]).wait()

    def x_step(s):
        o, yy = rank(s // 2), (y + s) % 2
        arrived(block(o, yy, 1 - x, c))
        to_c(o, yy, 1 - x).start()

    lead = 4
    for s in range(lead):
        x_step(s)
    own_weights.wait()
    weights_from(z, (1 - y,))
    weights_from(rank(1), (y, 1 - y))

    @pl.loop(0, NZ * NY)
    def _(s):
        @pl.when(s < NZ * NY - lead)
        def _():
            x_step(s + lead)

        o, yy = rank(s // 2), (y + s) % 2
        arrived(block(o, yy, x, 1 - c))
        arrived(block(o, yy, 1 - x, 1 - c))
        project(o * NY + yy, (0, 1), True, False)

    weights_from(rank(2), (y, 1 - y))
    weights_from(rank(3), (y, 1 - y))

    tap = [
        [taps[p, t : t + 1, pl.ds(own_lane, own)] for t in range(3)] for p in range(3)
    ]
    gain = skip[...]

    def features(q):
        start = 8 + q * rows
        feature = []
        for p in range(3):
            lanes = slice(p * own, (p + 1) * own)
            total = tap[p][0] * proj[start : start + rows, lanes]
            total = total + tap[p][1] * proj[start - 1 : start - 1 + rows, lanes]
            feature.append(total + tap[p][2] * proj[start - 2 : start - 2 + rows, lanes])
        gate[q * rows : (q + 1) * rows, :] = feature[0]
        n, at = q * rows // tile, q * rows % tile
        wave[at : at + rows, n * own : (n + 1) * own] = (feature[1] * feature[2]).astype(
            jnp.bfloat16
        )

    def multiply(n):
        lanes = [pl.ds(m * own, own) for m in range(n + 1)]

        @pl.loop(0, tile // 16, unroll=4)
        def _(step):
            re = pl.ds(pl.multiple_of(step * 16, 16), 16)
            im = pl.ds(pl.multiple_of(tile + step * 16, 16), 16)
            real, imag = 0.0, 0.0
            for m in range(n + 1):
                kr, ki = spectrum[re, lanes[n - m]], spectrum[im, lanes[n - m]]
                sr, si = signal[re, lanes[m]], signal[im, lanes[m]]
                real = real + (kr * sr - ki * si)
                imag = imag + (kr * si + ki * sr)
            product[re, :] = real.astype(jnp.bfloat16)
            product[im, :] = imag.astype(jnp.bfloat16)

    def out_push(q):
        return pltpu.make_async_remote_copy(
            src_ref=outgoing.at[q], dst_ref=out.at[pl.ds(own_lane, own), :],
            send_sem=o_send.at[q], recv_sem=o_recv.at[i],
            device_id=(q, j), device_id_type=MESH_ID,
        )

    def out_keep(q):
        return pltpu.make_async_copy(
            outgoing.at[q], out.at[pl.ds(own_lane, own), :], o_send.at[q]
        )

    per_tile = tile // rows
    for n in range(blocks):
        lanes = slice(n * own, (n + 1) * own)
        for half in range(per_tile):
            project(n * per_tile + half, (2, 3), False, True)
            features(n * per_tile + half)
        signal[:, lanes] = jnp.dot(
            forward[:, tile:], wave[:, lanes], preferred_element_type=jnp.float32
        )
        multiply(n)
        smeared = jnp.dot(inverse[...], product[...], preferred_element_type=jnp.float32)
        for half in range(per_tile):
            q = n * per_tile + half
            at = slice(half * rows, (half + 1) * rows)
            mixed = smeared[at] + gain * wave[at, lanes].astype(jnp.float32)
            mixed = mixed.astype(jnp.bfloat16).astype(jnp.float32)
            gated = gate[q * rows : (q + 1) * rows, :] * mixed
            outgoing[q] = gated.T.astype(jnp.bfloat16)

            @pl.when(i != q)
            def _():
                out_push(q).start()

            @pl.when(i == q)
            def _():
                out_keep(q).start()

    for o in range(NZ):
        @pl.when(jnp.logical_and(o <= z, z < NZ - 1))
        def _():
            up(o).wait_send()

        @pl.when(jnp.logical_and(o >= z, z > 0))
        def _():
            down(o).wait_send()

        to_y(o).wait_send()
        for yy in range(NY):
            to_x(o, yy).wait_send()
            for xx in range(NX):
                to_c(o, yy, xx).wait_send()
    for q in range(ctx_n):
        @pl.when(i != q)
        def _():
            weight_push(q).wait_send()
            out_push(q).wait_send()
            landed = out.at[pl.ds(q * own, own), :]
            pltpu.make_async_copy(landed, landed, o_recv.at[q]).wait()

        @pl.when(i == q)
        def _():
            out_keep(q).wait()


def fused_shards(tokens, in_weight, short_taps, long_filter, skip_gain):
    rows, depth = tokens.shape
    ctx_n, ch_n = NZ * NY, NX * NC
    own = long_filter.shape[1]
    span = rows * ctx_n
    tile = SPECTRAL
    lanes = span // tile * own
    forward, inverse = odd_frequency_tables(tile)
    vmem = pl.BlockSpec(memory_space=pltpu.VMEM)
    hbm = pl.BlockSpec(memory_space=pl.ANY)
    dma = pltpu.SemaphoreType.DMA
    flops = 2 * span * depth * ch_n * 3 * own
    return pl.pallas_call(
        mixer_kernel,
        out_shape=jax.ShapeDtypeStruct((ctx_n * own, rows), jnp.bfloat16),
        in_specs=[hbm, hbm, vmem, hbm, vmem, hbm, hbm],
        out_specs=hbm,
        scratch_shapes=[
            pltpu.VMEM(long_filter.shape, jnp.float32),
            pltpu.VMEM(forward.shape, jnp.bfloat16),
            pltpu.VMEM(inverse.shape, jnp.bfloat16),
            pltpu.VMEM((ctx_n * ch_n, rows, depth), jnp.bfloat16),
            pltpu.VMEM((ctx_n, in_weight.shape[1], 3 * own), jnp.bfloat16),
            pltpu.VMEM((depth * ch_n, 3 * own), jnp.bfloat16),
            pltpu.VMEM((8 + span, 3 * own), jnp.float32),
            pltpu.VMEM((2 * tile, lanes), jnp.float32),
            pltpu.VMEM((tile, lanes), jnp.bfloat16),
            pltpu.VMEM((2 * tile, lanes), jnp.float32),
            pltpu.VMEM((2 * tile, own), jnp.bfloat16),
            pltpu.VMEM((span, own), jnp.float32),
            pltpu.VMEM((ctx_n, own, rows), jnp.bfloat16),
            dma((6,)),
            dma((ctx_n * ch_n,)),
            dma((2 * NZ,)),
            dma((NZ,)),
            dma((ctx_n,)),
            dma((ctx_n * NX,)),
            dma((ctx_n,)),
            dma((ctx_n,)),
            dma((ctx_n,)),
            dma((ctx_n,)),
        ],
        compiler_params=pltpu.CompilerParams(
            collective_id=0, has_side_effects=True, vmem_limit_bytes=56 * 1024 * 1024
        ),
        cost_estimate=pl.CostEstimate(
            flops=flops, bytes_accessed=2 * tokens.size * ctx_n * ch_n, transcendentals=0
        ),
        name="mixer",
    )(tokens, in_weight, short_taps, long_filter, skip_gain, jnp.asarray(forward), jnp.asarray(inverse))


def fits(mesh, tokens, in_weight, long_filter):
    span, depth = tokens.shape
    return (
        dict(mesh.shape) == {"ctx": NZ * NY, "ch": NX * NC}
        and span == NZ * NY * 256
        and depth == NX * NC * 1024
        and in_weight.shape[2] == long_filter.shape[0] * long_filter.shape[1]
        and long_filter.shape[1] == NZ * NY * 128
    )


def solution(mesh):
    placed = (
        P("ctx", "ch"),
        P(None, "ctx", "ch"),
        P(None, None, "ch"),
        P("ch", "ctx", None),
        P("ch", "ctx"),
    )

    def run(tokens, in_weight, short_taps, long_filter, skip_gain):
        body = fused_shards if fits(mesh, tokens, in_weight, long_filter) else shards
        return jax.shard_map(
            body, mesh=mesh, in_specs=placed, out_specs=P("ch", "ctx"), check_vma=False
        )(tokens, in_weight, short_taps, long_filter, skip_gain)

    return run
```

```python
import math

import jax
import jax.numpy as jnp
import ml_dtypes
import numpy as np
from jax import lax
from jax.experimental import pallas as pl
from jax.experimental.pallas import tpu as pltpu
from jax.sharding import PartitionSpec as P

BLOCK = 1024


def shifted(block, axis, distance):
    devices = range(lax.axis_size(axis))
    route = [(i - distance, i) for i in devices if i - distance in devices]
    return lax.ppermute(block, axis, route)


def spectral_tables(tile_extent):
    period = 2 * tile_extent
    rows_in = jnp.arange(tile_extent, dtype=jnp.int32)[:, None]
    freq_index = jnp.arange(tile_extent, dtype=jnp.int32)
    first_slot = freq_index == 0
    phases = 2.0 * math.pi / period * (rows_in * freq_index[None, :] % period).astype(jnp.float32)
    top_phase = 2.0 * math.pi / period * (rows_in * tile_extent % period).astype(jnp.float32)
    forward_cos = jnp.cos(phases)
    forward_sin = jnp.where(first_slot[None, :], jnp.cos(top_phase), -jnp.sin(phases))
    times_out = jnp.arange(period, dtype=jnp.int32)[None, :]
    back_phases = (
        2.0 * math.pi / period * (freq_index[:, None] * times_out % period).astype(jnp.float32)
    )
    top_back = 2.0 * math.pi / period * (times_out * tile_extent % period).astype(jnp.float32)
    weights = jnp.where(first_slot, jnp.float32(1.0), jnp.float32(2.0)) / period
    inverse_cos = weights[:, None] * jnp.cos(back_phases)
    inverse_sin = jnp.where(
        first_slot[:, None], jnp.cos(top_back) / period, -(2.0 / period) * jnp.sin(back_phases)
    )
    return (forward_cos, forward_sin, inverse_cos, inverse_sin)


def global_causal_smear(gate_wave, kernel_table_lines, leftover_lines, tile_extent):
    lane_total, context_extent = gate_wave.shape
    tile_sequence_group = context_extent // tile_extent
    forward_cos, forward_sin, inverse_cos, inverse_sin = spectral_tables(tile_extent)
    first_slot = (jnp.arange(tile_extent, dtype=jnp.int32) == 0)[None, None, :]
    highest = lax.Precision.HIGHEST
    gate_wave_wide = gate_wave.astype(jnp.float32)
    source_wave = gate_wave_wide.reshape(lane_total, tile_sequence_group, tile_extent)
    kernel = kernel_table_lines.reshape(lane_total, tile_sequence_group, tile_extent)
    signal_real = jnp.einsum("cnb,bf->cnf", source_wave, forward_cos, precision=highest)
    signal_imag = jnp.einsum("cnb,bf->cnf", source_wave, forward_sin, precision=highest)
    kernel_real = jnp.einsum("cnb,bf->cnf", kernel, forward_cos, precision=highest)
    kernel_imag = jnp.einsum("cnb,bf->cnf", kernel, forward_sin, precision=highest)
    zeros_pad = jnp.zeros((lane_total, tile_sequence_group, tile_extent), jnp.float32)
    padded_real = jnp.concatenate([zeros_pad, signal_real], axis=1)
    padded_imag = jnp.concatenate([zeros_pad, signal_imag], axis=1)

    def accumulate(offset, totals):
        total_real, total_imag = totals
        shifted_real = lax.dynamic_slice_in_dim(
            padded_real, tile_sequence_group - offset, tile_sequence_group, 1
        )
        shifted_imag = lax.dynamic_slice_in_dim(
            padded_imag, tile_sequence_group - offset, tile_sequence_group, 1
        )
        filter_real = lax.dynamic_slice_in_dim(kernel_real, offset, 1, 1)
        filter_imag = lax.dynamic_slice_in_dim(kernel_imag, offset, 1, 1)
        cross = filter_imag * shifted_imag
        next_real = (
            total_real + filter_real * shifted_real - jnp.where(first_slot, jnp.float32(0.0), cross)
        )
        next_imag = total_imag + jnp.where(
            first_slot, cross, filter_real * shifted_imag + filter_imag * shifted_real
        )
        return (next_real, next_imag)

    total_real, total_imag = lax.fori_loop(
        0, tile_sequence_group, accumulate, (zeros_pad, zeros_pad)
    )
    inverse_rows = jnp.einsum("cnf,ft->cnt", total_real, inverse_cos, precision=highest)
    inverse_rows = inverse_rows + jnp.einsum(
        "cnf,ft->cnt", total_imag, inverse_sin, precision=highest
    )
    front_half = inverse_rows[:, :, :tile_extent]
    back_half = inverse_rows[:, :, tile_extent:]
    carried = jnp.concatenate(
        [jnp.zeros((lane_total, 1, tile_extent), jnp.float32), back_half[:, :-1]], axis=1
    )
    affine_mapping = (front_half + carried).reshape(lane_total, context_extent)
    return (affine_mapping + leftover_lines[:, None] * gate_wave_wide).astype(jnp.bfloat16)


def short_conv(projected_float, local_taps, previous):
    context_extent = projected_float.shape[2]
    extended = jnp.concatenate([previous, projected_float], axis=2)
    result = jnp.zeros_like(projected_float)
    for offset in range(3):
        result = (
            result
            + local_taps[:, offset, :][:, :, None]
            * extended[:, :, 2 - offset : 2 - offset + context_extent]
        )
    return result


def shards(tokens, in_weight, short_taps, long_filter, skip_gain):
    whole_tokens = lax.all_gather(tokens, "ch", axis=1, tiled=True)
    local_tokens = whole_tokens.shape[0]
    summed = jnp.einsum(
        "pdc,ld->pcl",
        lax.all_gather(in_weight, "ctx", axis=1, tiled=True),
        whole_tokens,
        preferred_element_type=jnp.float32,
    )
    projected = summed.astype(jnp.bfloat16)
    kernel_table_lines = long_filter[0]
    leftover_lines = skip_gain[0]
    last_rows = projected[:, :, local_tokens - 2 :]
    previous = shifted(last_rows, "ctx", 1)
    embedding_result = short_conv(
        projected.astype(jnp.float32), short_taps, previous.astype(jnp.float32)
    )
    gate_wave = (embedding_result[1] * embedding_result[2]).astype(jnp.bfloat16)
    per_channel_view = lax.all_to_all(gate_wave, "ctx", split_axis=0, concat_axis=1, tiled=True)
    blended_lines = global_causal_smear(per_channel_view, kernel_table_lines, leftover_lines, BLOCK)
    by_token = lax.all_to_all(blended_lines, "ctx", split_axis=1, concat_axis=0, tiled=True)
    gated_output = (embedding_result[0] * by_token.astype(jnp.float32)).astype(jnp.bfloat16)
    return gated_output


NZ, NY, NX, NC = 4, 2, 2, 2
SPECTRAL = 512
MESH_ID = pl.DeviceIdType.MESH


def odd_frequency_tables(tile):
    odd = 2 * np.arange(tile, dtype=np.int64) + 1
    turns = 2.0 * np.pi / (4 * tile)
    times = np.arange(-tile, tile, dtype=np.int64)
    phase = turns * ((odd[:, None] * times[None, :]) % (4 * tile))
    forward = np.concatenate([np.cos(phase), -np.sin(phase)], axis=0)
    back = turns * ((np.arange(tile, dtype=np.int64)[:, None] * odd[None, :]) % (4 * tile))
    inverse = np.concatenate([np.cos(back), -np.sin(back)], axis=1) / tile
    return forward.astype(ml_dtypes.bfloat16), inverse.astype(ml_dtypes.bfloat16)


def mixer_kernel(
    tokens, weight, taps, filters_in, skip, forward_in, inverse_in, out,
    filters, forward, inverse, tok, wsend, wbuf, proj, spectrum, wave, signal, product, gate, outgoing,
    local_sem, tok_recv, z_send, y_send, x_send, c_send, w_recv, w_send, o_recv, o_send,
):
    ctx_n = NZ * NY
    rows, depth = tokens.shape
    w_depth = weight.shape[1]
    own = filters.shape[1]
    staged = ((filters_in, filters), (forward_in, forward), (inverse_in, inverse))
    tile = SPECTRAL
    blocks = rows * ctx_n // tile
    i, j = lax.axis_index("ctx"), lax.axis_index("ch")
    z, y = i // NY, i % NY
    x, c = j // NC, j % NC
    low = z // 2

    def device(zz, yy, xx, cc):
        return (zz * NY + yy, xx * NC + cc)

    def block(zz, yy, xx, cc):
        return (zz * NY + yy) * (NX * NC) + xx * NC + cc

    def push(b, sem, target):
        return pltpu.make_async_remote_copy(
            src_ref=tok.at[b], dst_ref=tok.at[b], send_sem=sem, recv_sem=tok_recv.at[b],
            device_id=target, device_id_type=MESH_ID,
        )

    def up(o):
        return push(block(o, y, x, c), z_send.at[o], device(z + 1, y, x, c))

    def down(o):
        return push(block(o, y, x, c), z_send.at[NZ + o], device(z - 1, y, x, c))

    def to_y(o):
        return push(block(o, y, x, c), y_send.at[o], device(z, 1 - y, x, c))

    def to_x(o, yy):
        return push(block(o, yy, x, c), x_send.at[o * NY + yy], device(z, y, 1 - x, c))

    def to_c(o, yy, xx):
        return push(
            block(o, yy, xx, c), c_send.at[(o * NY + yy) * NX + xx], device(z, y, x, 1 - c)
        )

    def arrived(b):
        pltpu.make_async_copy(tok.at[b], tok.at[b], tok_recv.at[b]).wait()

    def rank(r):
        g = r // 2
        return (1 - g) * (z + r * (1 - 2 * (z % 2))) + g * (r + low * (3 - 2 * r))

    barrier = pltpu.get_barrier_semaphore()
    for k in range(1, ctx_n):
        pl.semaphore_signal(
            barrier, inc=1, device_id=((i + k) % ctx_n, j), device_id_type=MESH_ID
        )
    for target in (device(z, y, 1 - x, c), device(z, y, x, 1 - c)):
        pl.semaphore_signal(barrier, inc=1, device_id=target, device_id_type=MESH_ID)
    mine = block(z, y, x, c)
    first = pltpu.make_async_copy(tokens, tok.at[mine], local_sem.at[0])
    first.start()
    own_row = pl.multiple_of(i * w_depth, w_depth)
    own_lane = pl.multiple_of(i * own, own)
    for peer in range(ctx_n):
        for p in range(3):
            pltpu.make_async_copy(
                weight.at[p, :, pl.ds(peer * own, own)],
                wsend.at[peer, :, pl.ds(p * own, own)],
                local_sem.at[1],
            ).start()
    for k, (src, dst) in enumerate(staged):
        pltpu.make_async_copy(src, dst, local_sem.at[2 + k]).start()
    first.wait()
    pl.semaphore_wait(barrier, ctx_n + 1)

    @pl.when(z < NZ - 1)
    def _():
        up(z).start()

    @pl.when(z > 0)
    def _():
        down(z).start()

    to_y(z).start()
    to_x(z, y).start()
    to_c(z, y, x).start()

    def weight_push(peer):
        return pltpu.make_async_remote_copy(
            src_ref=wsend.at[peer], dst_ref=wbuf.at[pl.ds(own_row, w_depth), :],
            send_sem=w_send.at[peer], recv_sem=w_recv.at[i],
            device_id=(peer, j), device_id_type=MESH_ID,
        )

    def push_weights(zz, ys):
        for yy in ys:
            weight_push(zz * NY + yy).start()

    def z_step(r):
        o = rank(r)
        arrived(block(o, y, x, c))

        @pl.when(jnp.logical_and(o < z, z < NZ - 1))
        def _():
            up(o).start()

        @pl.when(jnp.logical_and(o > z, z > 0))
        def _():
            down(o).start()

        to_y(o).start()
        to_x(o, y).start()
        to_c(o, y, x).start()

    def y_step(r):
        o = rank(r)
        arrived(block(o, 1 - y, x, c))
        to_x(o, 1 - y).start()
        to_c(o, 1 - y, x).start()

    for k, (src, dst) in enumerate(staged):
        pltpu.make_async_copy(src, dst, local_sem.at[2 + k]).wait()

    for n in range(blocks):
        lo = max(n - 1, 0) * tile
        window = filters[0, :, lo : (n + 1) * tile].astype(jnp.bfloat16)
        table = forward[:, tile:] if n == 0 else forward[...]
        spectrum[:, n * own : (n + 1) * own] = lax.dot_general(
            table, window, (((1,), (1,)), ((), ())), preferred_element_type=jnp.float32
        )

    pltpu.make_async_copy(wsend, wsend, local_sem.at[1]).wait()
    own_weights = pltpu.make_async_copy(
        wsend.at[i], wbuf.at[pl.ds(own_row, w_depth), :], local_sem.at[5]
    )
    own_weights.start()

    z_step(1)
    y_step(0)
    push_weights(z, (1 - y,))
    z_step(2)
    push_weights(rank(3), (y, 1 - y))
    y_step(1)
    z_step(3)
    push_weights(rank(2), (y, 1 - y))
    y_step(2)
    push_weights(rank(1), (y, 1 - y))
    y_step(3)

    proj[0:8, :] = jnp.zeros((8, 3 * own), jnp.float32)

    def project(at, ranks, begin, end):
        row = pl.multiple_of(8 + at * rows, 8)
        total = None if begin else proj[pl.ds(row, rows), :]
        for r in ranks:
            q = rank(r)
            part = jnp.dot(
                tok[at * (NX * NC) + q],
                wbuf[pl.ds(pl.multiple_of(q * depth, depth), depth), :],
                preferred_element_type=jnp.float32,
            )
            total = part if total is None else total + part
        if end:
            total = total.astype(jnp.bfloat16).astype(jnp.float32)
        proj[pl.ds(row, rows), :] = total

    def weights_from(zz, ys):
        for yy in ys:
            peer = zz * NY + yy
            piece = wbuf.at[pl.ds(pl.multiple_of(peer * w_depth, w_depth), w_depth), :]
            pltpu.make_async_copy(piece, piece, w_recv.at[peer]).wait()

    def x_step(s):
        o, yy = rank(s // 2), (y + s) % 2
        arrived(block(o, yy, 1 - x, c))
        to_c(o, yy, 1 - x).start()

    lead = 4
    for s in range(lead):
        x_step(s)
    own_weights.wait()
    weights_from(z, (1 - y,))
    weights_from(rank(1), (y, 1 - y))

    def place(s):
        return rank(s // 2) * NY + (y + s) % 2

    def complete(s):
        o, yy = rank(s // 2), (y + s) % 2
        arrived(block(o, yy, x, 1 - c))
        arrived(block(o, yy, 1 - x, 1 - c))

    early = NZ * NY - NY

    @pl.loop(0, early)
    def _(s):
        @pl.when(s < NZ * NY - lead)
        def _():
            x_step(s + lead)

        complete(s)
        project(place(s), (0, 1), True, False)

    weights_from(rank(3), (y, 1 - y))

    @pl.loop(0, early)
    def _(s):
        project(place(s), (3,), False, False)

    weights_from(rank(2), (y, 1 - y))

    @pl.loop(0, early)
    def _(s):
        project(place(s), (2,), False, True)

    @pl.loop(early, NZ * NY)
    def _(s):
        complete(s)
        project(place(s), (0, 1, 3, 2), True, True)

    tap = [
        [taps[p, t : t + 1, pl.ds(own_lane, own)] for t in range(3)] for p in range(3)
    ]
    gain = skip[...]

    def features(q):
        start = 8 + q * rows
        feature = []
        for p in range(3):
            lanes = slice(p * own, (p + 1) * own)
            total = tap[p][0] * proj[start : start + rows, lanes]
            total = total + tap[p][1] * proj[start - 1 : start - 1 + rows, lanes]
            feature.append(total + tap[p][2] * proj[start - 2 : start - 2 + rows, lanes])
        gate[q * rows : (q + 1) * rows, :] = feature[0]
        n, at = q * rows // tile, q * rows % tile
        wave[at : at + rows, n * own : (n + 1) * own] = (feature[1] * feature[2]).astype(
            jnp.bfloat16
        )

    def multiply(n):
        lanes = [pl.ds(m * own, own) for m in range(n + 1)]

        @pl.loop(0, tile // 16, unroll=4)
        def _(step):
            re = pl.ds(pl.multiple_of(step * 16, 16), 16)
            im = pl.ds(pl.multiple_of(tile + step * 16, 16), 16)
            real, imag = 0.0, 0.0
            for m in range(n + 1):
                kr, ki = spectrum[re, lanes[n - m]], spectrum[im, lanes[n - m]]
                sr, si = signal[re, lanes[m]], signal[im, lanes[m]]
                real = real + (kr * sr - ki * si)
                imag = imag + (kr * si + ki * sr)
            product[re, :] = real.astype(jnp.bfloat16)
            product[im, :] = imag.astype(jnp.bfloat16)

    def out_push(q):
        return pltpu.make_async_remote_copy(
            src_ref=outgoing.at[q], dst_ref=out.at[pl.ds(own_lane, own), :],
            send_sem=o_send.at[q], recv_sem=o_recv.at[i],
            device_id=(q, j), device_id_type=MESH_ID,
        )

    def out_keep(q):
        return pltpu.make_async_copy(
            outgoing.at[q], out.at[pl.ds(own_lane, own), :], o_send.at[q]
        )

    per_tile = tile // rows
    for n in range(blocks):
        lanes = slice(n * own, (n + 1) * own)
        for half in range(per_tile):
            features(n * per_tile + half)
        signal[:, lanes] = jnp.dot(
            forward[:, tile:], wave[:, lanes], preferred_element_type=jnp.float32
        )
        multiply(n)
        smeared = jnp.dot(inverse[...], product[...], preferred_element_type=jnp.float32)
        for half in range(per_tile):
            q = n * per_tile + half
            at = slice(half * rows, (half + 1) * rows)
            mixed = smeared[at] + gain * wave[at, lanes].astype(jnp.float32)
            mixed = mixed.astype(jnp.bfloat16).astype(jnp.float32)
            gated = gate[q * rows : (q + 1) * rows, :] * mixed
            outgoing[q] = gated.T.astype(jnp.bfloat16)

            @pl.when(i != q)
            def _():
                out_push(q).start()

            @pl.when(i == q)
            def _():
                out_keep(q).start()

    for o in range(NZ):
        @pl.when(jnp.logical_and(o <= z, z < NZ - 1))
        def _():
            up(o).wait_send()

        @pl.when(jnp.logical_and(o >= z, z > 0))
        def _():
            down(o).wait_send()

        to_y(o).wait_send()
        for yy in range(NY):
            to_x(o, yy).wait_send()
            for xx in range(NX):
                to_c(o, yy, xx).wait_send()
    for q in range(ctx_n):
        @pl.when(i != q)
        def _():
            weight_push(q).wait_send()
            out_push(q).wait_send()
            landed = out.at[pl.ds(q * own, own), :]
            pltpu.make_async_copy(landed, landed, o_recv.at[q]).wait()

        @pl.when(i == q)
        def _():
            out_keep(q).wait()


def fused_shards(tokens, in_weight, short_taps, long_filter, skip_gain):
    rows, depth = tokens.shape
    ctx_n, ch_n = NZ * NY, NX * NC
    own = long_filter.shape[1]
    span = rows * ctx_n
    tile = SPECTRAL
    lanes = span // tile * own
    forward, inverse = odd_frequency_tables(tile)
    vmem = pl.BlockSpec(memory_space=pltpu.VMEM)
    hbm = pl.BlockSpec(memory_space=pl.ANY)
    dma = pltpu.SemaphoreType.DMA
    flops = 2 * span * depth * ch_n * 3 * own
    return pl.pallas_call(
        mixer_kernel,
        out_shape=jax.ShapeDtypeStruct((ctx_n * own, rows), jnp.bfloat16),
        in_specs=[hbm, hbm, vmem, hbm, vmem, hbm, hbm],
        out_specs=hbm,
        scratch_shapes=[
            pltpu.VMEM(long_filter.shape, jnp.float32),
            pltpu.VMEM(forward.shape, jnp.bfloat16),
            pltpu.VMEM(inverse.shape, jnp.bfloat16),
            pltpu.VMEM((ctx_n * ch_n, rows, depth), jnp.bfloat16),
            pltpu.VMEM((ctx_n, in_weight.shape[1], 3 * own), jnp.bfloat16),
            pltpu.VMEM((depth * ch_n, 3 * own), jnp.bfloat16),
            pltpu.VMEM((8 + span, 3 * own), jnp.float32),
            pltpu.VMEM((2 * tile, lanes), jnp.float32),
            pltpu.VMEM((tile, lanes), jnp.bfloat16),
            pltpu.VMEM((2 * tile, lanes), jnp.float32),
            pltpu.VMEM((2 * tile, own), jnp.bfloat16),
            pltpu.VMEM((span, own), jnp.float32),
            pltpu.VMEM((ctx_n, own, rows), jnp.bfloat16),
            dma((6,)),
            dma((ctx_n * ch_n,)),
            dma((2 * NZ,)),
            dma((NZ,)),
            dma((ctx_n,)),
            dma((ctx_n * NX,)),
            dma((ctx_n,)),
            dma((ctx_n,)),
            dma((ctx_n,)),
            dma((ctx_n,)),
        ],
        compiler_params=pltpu.CompilerParams(
            collective_id=0, has_side_effects=True, vmem_limit_bytes=56 * 1024 * 1024
        ),
        cost_estimate=pl.CostEstimate(
            flops=flops, bytes_accessed=2 * tokens.size * ctx_n * ch_n, transcendentals=0
        ),
        name="mixer",
    )(tokens, in_weight, short_taps, long_filter, skip_gain, jnp.asarray(forward), jnp.asarray(inverse))


def fits(mesh, tokens, in_weight, long_filter):
    span, depth = tokens.shape
    return (
        dict(mesh.shape) == {"ctx": NZ * NY, "ch": NX * NC}
        and span == NZ * NY * 256
        and depth == NX * NC * 1024
        and in_weight.shape[2] == long_filter.shape[0] * long_filter.shape[1]
        and long_filter.shape[1] == NZ * NY * 128
    )


def solution(mesh):
    placed = (
        P("ctx", "ch"),
        P(None, "ctx", "ch"),
        P(None, None, "ch"),
        P("ch", "ctx", None),
        P("ch", "ctx"),
    )

    def run(tokens, in_weight, short_taps, long_filter, skip_gain):
        body = fused_shards if fits(mesh, tokens, in_weight, long_filter) else shards
        return jax.shard_map(
            body, mesh=mesh, in_specs=placed, out_specs=P("ch", "ctx"), check_vma=False
        )(tokens, in_weight, short_taps, long_filter, skip_gain)

    return run
```

```python
import math

import jax
import jax.numpy as jnp
import ml_dtypes
import numpy as np
from jax import lax
from jax.experimental import pallas as pl
from jax.experimental.pallas import tpu as pltpu
from jax.sharding import PartitionSpec as P

BLOCK = 1024


def shifted(block, axis, distance):
    devices = range(lax.axis_size(axis))
    route = [(i - distance, i) for i in devices if i - distance in devices]
    return lax.ppermute(block, axis, route)


def spectral_tables(tile_extent):
    period = 2 * tile_extent
    rows_in = jnp.arange(tile_extent, dtype=jnp.int32)[:, None]
    freq_index = jnp.arange(tile_extent, dtype=jnp.int32)
    first_slot = freq_index == 0
    phases = 2.0 * math.pi / period * (rows_in * freq_index[None, :] % period).astype(jnp.float32)
    top_phase = 2.0 * math.pi / period * (rows_in * tile_extent % period).astype(jnp.float32)
    forward_cos = jnp.cos(phases)
    forward_sin = jnp.where(first_slot[None, :], jnp.cos(top_phase), -jnp.sin(phases))
    times_out = jnp.arange(period, dtype=jnp.int32)[None, :]
    back_phases = (
        2.0 * math.pi / period * (freq_index[:, None] * times_out % period).astype(jnp.float32)
    )
    top_back = 2.0 * math.pi / period * (times_out * tile_extent % period).astype(jnp.float32)
    weights = jnp.where(first_slot, jnp.float32(1.0), jnp.float32(2.0)) / period
    inverse_cos = weights[:, None] * jnp.cos(back_phases)
    inverse_sin = jnp.where(
        first_slot[:, None], jnp.cos(top_back) / period, -(2.0 / period) * jnp.sin(back_phases)
    )
    return (forward_cos, forward_sin, inverse_cos, inverse_sin)


def global_causal_smear(gate_wave, kernel_table_lines, leftover_lines, tile_extent):
    lane_total, context_extent = gate_wave.shape
    tile_sequence_group = context_extent // tile_extent
    forward_cos, forward_sin, inverse_cos, inverse_sin = spectral_tables(tile_extent)
    first_slot = (jnp.arange(tile_extent, dtype=jnp.int32) == 0)[None, None, :]
    highest = lax.Precision.HIGHEST
    gate_wave_wide = gate_wave.astype(jnp.float32)
    source_wave = gate_wave_wide.reshape(lane_total, tile_sequence_group, tile_extent)
    kernel = kernel_table_lines.reshape(lane_total, tile_sequence_group, tile_extent)
    signal_real = jnp.einsum("cnb,bf->cnf", source_wave, forward_cos, precision=highest)
    signal_imag = jnp.einsum("cnb,bf->cnf", source_wave, forward_sin, precision=highest)
    kernel_real = jnp.einsum("cnb,bf->cnf", kernel, forward_cos, precision=highest)
    kernel_imag = jnp.einsum("cnb,bf->cnf", kernel, forward_sin, precision=highest)
    zeros_pad = jnp.zeros((lane_total, tile_sequence_group, tile_extent), jnp.float32)
    padded_real = jnp.concatenate([zeros_pad, signal_real], axis=1)
    padded_imag = jnp.concatenate([zeros_pad, signal_imag], axis=1)

    def accumulate(offset, totals):
        total_real, total_imag = totals
        shifted_real = lax.dynamic_slice_in_dim(
            padded_real, tile_sequence_group - offset, tile_sequence_group, 1
        )
        shifted_imag = lax.dynamic_slice_in_dim(
            padded_imag, tile_sequence_group - offset, tile_sequence_group, 1
        )
        filter_real = lax.dynamic_slice_in_dim(kernel_real, offset, 1, 1)
        filter_imag = lax.dynamic_slice_in_dim(kernel_imag, offset, 1, 1)
        cross = filter_imag * shifted_imag
        next_real = (
            total_real + filter_real * shifted_real - jnp.where(first_slot, jnp.float32(0.0), cross)
        )
        next_imag = total_imag + jnp.where(
            first_slot, cross, filter_real * shifted_imag + filter_imag * shifted_real
        )
        return (next_real, next_imag)

    total_real, total_imag = lax.fori_loop(
        0, tile_sequence_group, accumulate, (zeros_pad, zeros_pad)
    )
    inverse_rows = jnp.einsum("cnf,ft->cnt", total_real, inverse_cos, precision=highest)
    inverse_rows = inverse_rows + jnp.einsum(
        "cnf,ft->cnt", total_imag, inverse_sin, precision=highest
    )
    front_half = inverse_rows[:, :, :tile_extent]
    back_half = inverse_rows[:, :, tile_extent:]
    carried = jnp.concatenate(
        [jnp.zeros((lane_total, 1, tile_extent), jnp.float32), back_half[:, :-1]], axis=1
    )
    affine_mapping = (front_half + carried).reshape(lane_total, context_extent)
    return (affine_mapping + leftover_lines[:, None] * gate_wave_wide).astype(jnp.bfloat16)


def short_conv(projected_float, local_taps, previous):
    context_extent = projected_float.shape[2]
    extended = jnp.concatenate([previous, projected_float], axis=2)
    result = jnp.zeros_like(projected_float)
    for offset in range(3):
        result = (
            result
            + local_taps[:, offset, :][:, :, None]
            * extended[:, :, 2 - offset : 2 - offset + context_extent]
        )
    return result


def shards(tokens, in_weight, short_taps, long_filter, skip_gain):
    whole_tokens = lax.all_gather(tokens, "ch", axis=1, tiled=True)
    local_tokens = whole_tokens.shape[0]
    summed = jnp.einsum(
        "pdc,ld->pcl",
        lax.all_gather(in_weight, "ctx", axis=1, tiled=True),
        whole_tokens,
        preferred_element_type=jnp.float32,
    )
    projected = summed.astype(jnp.bfloat16)
    kernel_table_lines = long_filter[0]
    leftover_lines = skip_gain[0]
    last_rows = projected[:, :, local_tokens - 2 :]
    previous = shifted(last_rows, "ctx", 1)
    embedding_result = short_conv(
        projected.astype(jnp.float32), short_taps, previous.astype(jnp.float32)
    )
    gate_wave = (embedding_result[1] * embedding_result[2]).astype(jnp.bfloat16)
    per_channel_view = lax.all_to_all(gate_wave, "ctx", split_axis=0, concat_axis=1, tiled=True)
    blended_lines = global_causal_smear(per_channel_view, kernel_table_lines, leftover_lines, BLOCK)
    by_token = lax.all_to_all(blended_lines, "ctx", split_axis=1, concat_axis=0, tiled=True)
    gated_output = (embedding_result[0] * by_token.astype(jnp.float32)).astype(jnp.bfloat16)
    return gated_output


NZ, NY, NX, NC = 4, 2, 2, 2
SPECTRAL = 512
MESH_ID = pl.DeviceIdType.MESH


def odd_frequency_tables(tile):
    odd = 2 * np.arange(tile, dtype=np.int64) + 1
    turns = 2.0 * np.pi / (4 * tile)
    times = np.arange(-tile, tile, dtype=np.int64)
    phase = turns * ((odd[:, None] * times[None, :]) % (4 * tile))
    forward = np.concatenate([np.cos(phase), -np.sin(phase)], axis=0)
    back = turns * ((np.arange(tile, dtype=np.int64)[:, None] * odd[None, :]) % (4 * tile))
    inverse = np.concatenate([np.cos(back), -np.sin(back)], axis=1) / tile
    return forward.astype(ml_dtypes.bfloat16), inverse.astype(ml_dtypes.bfloat16)


def mixer_kernel(
    tokens, weight, taps, filters_in, skip, forward_in, inverse_in, out,
    filters, forward, inverse, tok, wsend, wbuf, proj, spectrum, wave, signal, product, gate, outgoing,
    local_sem, tok_recv, z_send, y_send, x_send, c_send, w_recv, w_send, o_recv, o_send,
):
    ctx_n = NZ * NY
    rows, depth = tokens.shape
    w_depth = weight.shape[1]
    own = filters.shape[1]
    staged = ((filters_in, filters), (forward_in, forward), (inverse_in, inverse))
    tile = SPECTRAL
    blocks = rows * ctx_n // tile
    i, j = lax.axis_index("ctx"), lax.axis_index("ch")
    z, y = i // NY, i % NY
    x, c = j // NC, j % NC
    low = z // 2

    def device(zz, yy, xx, cc):
        return (zz * NY + yy, xx * NC + cc)

    def block(zz, yy, xx, cc):
        return (zz * NY + yy) * (NX * NC) + xx * NC + cc

    half_rows = rows // 2
    halves = (0, 1)

    def part(b, h):
        return tok.at[b, pl.ds(h * half_rows, half_rows)]

    def push(b, h, sem, target):
        return pltpu.make_async_remote_copy(
            src_ref=part(b, h), dst_ref=part(b, h), send_sem=sem, recv_sem=tok_recv.at[2 * b + h],
            device_id=target, device_id_type=MESH_ID,
        )

    def up(o, h):
        return push(block(o, y, x, c), h, z_send.at[2 * o + h], device(z + 1, y, x, c))

    def down(o, h):
        return push(
            block(o, y, x, c), h, z_send.at[2 * (NZ + o) + h], device(z - 1, y, x, c)
        )

    def to_y(o, h):
        return push(block(o, y, x, c), h, y_send.at[2 * o + h], device(z, 1 - y, x, c))

    def to_x(o, yy, h):
        return push(
            block(o, yy, x, c), h, x_send.at[2 * (o * NY + yy) + h], device(z, y, 1 - x, c)
        )

    def to_c(o, yy, xx):
        b = block(o, yy, xx, c)
        return pltpu.make_async_remote_copy(
            src_ref=tok.at[b], dst_ref=tok.at[b],
            send_sem=c_send.at[(o * NY + yy) * NX + xx], recv_sem=tok_recv.at[2 * b],
            device_id=device(z, y, x, 1 - c), device_id_type=MESH_ID,
        )

    def arrived(b, h):
        pltpu.make_async_copy(part(b, h), part(b, h), tok_recv.at[2 * b + h]).wait()

    def arrived_whole(b):
        pltpu.make_async_copy(tok.at[b], tok.at[b], tok_recv.at[2 * b]).wait()

    def rank(r):
        g = r // 2
        return (1 - g) * (z + r * (1 - 2 * (z % 2))) + g * (r + low * (3 - 2 * r))

    barrier = pltpu.get_barrier_semaphore()
    for k in range(1, ctx_n):
        pl.semaphore_signal(
            barrier, inc=1, device_id=((i + k) % ctx_n, j), device_id_type=MESH_ID
        )
    for target in (device(z, y, 1 - x, c), device(z, y, x, 1 - c)):
        pl.semaphore_signal(barrier, inc=1, device_id=target, device_id_type=MESH_ID)
    mine = block(z, y, x, c)
    first = pltpu.make_async_copy(tokens, tok.at[mine], local_sem.at[0])
    first.start()
    own_row = pl.multiple_of(i * w_depth, w_depth)
    own_lane = pl.multiple_of(i * own, own)
    for peer in range(ctx_n):
        for p in range(3):
            pltpu.make_async_copy(
                weight.at[p, :, pl.ds(peer * own, own)],
                wsend.at[peer, :, pl.ds(p * own, own)],
                local_sem.at[1],
            ).start()
    for k, (src, dst) in enumerate(staged):
        pltpu.make_async_copy(src, dst, local_sem.at[2 + k]).start()
    first.wait()
    pl.semaphore_wait(barrier, ctx_n + 1)

    for h in halves:
        @pl.when(z < NZ - 1)
        def _():
            up(z, h).start()

        @pl.when(z > 0)
        def _():
            down(z, h).start()

        to_y(z, h).start()
        to_x(z, y, h).start()
    to_c(z, y, x).start()

    def weight_push(peer):
        return pltpu.make_async_remote_copy(
            src_ref=wsend.at[peer], dst_ref=wbuf.at[pl.ds(own_row, w_depth), :],
            send_sem=w_send.at[peer], recv_sem=w_recv.at[i],
            device_id=(peer, j), device_id_type=MESH_ID,
        )

    def push_weights(zz, ys):
        for yy in ys:
            weight_push(zz * NY + yy).start()

    def z_step(r):
        o = rank(r)
        for h in halves:
            arrived(block(o, y, x, c), h)

            @pl.when(jnp.logical_and(o < z, z < NZ - 1))
            def _():
                up(o, h).start()

            @pl.when(jnp.logical_and(o > z, z > 0))
            def _():
                down(o, h).start()

            to_y(o, h).start()
            to_x(o, y, h).start()
        to_c(o, y, x).start()

    def y_step(r):
        o = rank(r)
        for h in halves:
            arrived(block(o, 1 - y, x, c), h)
            to_x(o, 1 - y, h).start()
        to_c(o, 1 - y, x).start()

    for k, (src, dst) in enumerate(staged):
        pltpu.make_async_copy(src, dst, local_sem.at[2 + k]).wait()

    for n in range(blocks):
        lo = max(n - 1, 0) * tile
        window = filters[0, :, lo : (n + 1) * tile].astype(jnp.bfloat16)
        table = forward[:, tile:] if n == 0 else forward[...]
        spectrum[:, n * own : (n + 1) * own] = lax.dot_general(
            table, window, (((1,), (1,)), ((), ())), preferred_element_type=jnp.float32
        )

    pltpu.make_async_copy(wsend, wsend, local_sem.at[1]).wait()
    own_weights = pltpu.make_async_copy(
        wsend.at[i], wbuf.at[pl.ds(own_row, w_depth), :], local_sem.at[5]
    )
    own_weights.start()

    z_step(1)
    y_step(0)
    push_weights(z, (1 - y,))
    z_step(2)
    push_weights(rank(3), (y, 1 - y))
    y_step(1)
    z_step(3)
    push_weights(rank(2), (y, 1 - y))
    y_step(2)
    push_weights(rank(1), (y, 1 - y))
    y_step(3)

    proj[0:8, :] = jnp.zeros((8, 3 * own), jnp.float32)

    def project(at, ranks, begin, end):
        row = 8 + at * rows if isinstance(at, int) else pl.multiple_of(8 + at * rows, 8)
        total = None if begin else proj[pl.ds(row, rows), :]
        for r in ranks:
            q = rank(r)
            part = jnp.dot(
                tok[at * (NX * NC) + q],
                wbuf[pl.ds(pl.multiple_of(q * depth, depth), depth), :],
                preferred_element_type=jnp.float32,
            )
            total = part if total is None else total + part
        if end:
            total = total.astype(jnp.bfloat16).astype(jnp.float32)
        proj[pl.ds(row, rows), :] = total

    def weights_from(zz, ys):
        for yy in ys:
            peer = zz * NY + yy
            piece = wbuf.at[pl.ds(pl.multiple_of(peer * w_depth, w_depth), w_depth), :]
            pltpu.make_async_copy(piece, piece, w_recv.at[peer]).wait()

    def x_step(s):
        o, yy = rank(s // 2), (y + s) % 2
        for h in halves:
            arrived(block(o, yy, 1 - x, c), h)
        to_c(o, yy, 1 - x).start()

    lead = 4
    for s in range(lead):
        x_step(s)
    own_weights.wait()
    weights_from(z, (1 - y,))
    weights_from(rank(1), (y, 1 - y))

    @pl.loop(0, NZ * NY)
    def _(s):
        @pl.when(s < NZ * NY - lead)
        def _():
            x_step(s + lead)

        o, yy = rank(s // 2), (y + s) % 2
        arrived_whole(block(o, yy, x, 1 - c))
        arrived_whole(block(o, yy, 1 - x, 1 - c))
        project(o * NY + yy, (0, 1), True, False)

    weights_from(rank(2), (y, 1 - y))
    weights_from(rank(3), (y, 1 - y))

    tap = [
        [taps[p, t : t + 1, pl.ds(own_lane, own)] for t in range(3)] for p in range(3)
    ]
    gain = skip[...]

    def features(q):
        start = 8 + q * rows
        feature = []
        for p in range(3):
            lanes = slice(p * own, (p + 1) * own)
            total = tap[p][0] * proj[start : start + rows, lanes]
            total = total + tap[p][1] * proj[start - 1 : start - 1 + rows, lanes]
            feature.append(total + tap[p][2] * proj[start - 2 : start - 2 + rows, lanes])
        gate[q * rows : (q + 1) * rows, :] = feature[0]
        n, at = q * rows // tile, q * rows % tile
        wave[at : at + rows, n * own : (n + 1) * own] = (feature[1] * feature[2]).astype(
            jnp.bfloat16
        )

    def multiply(n):
        lanes = [pl.ds(m * own, own) for m in range(n + 1)]

        @pl.loop(0, tile // 16, unroll=4)
        def _(step):
            re = pl.ds(pl.multiple_of(step * 16, 16), 16)
            im = pl.ds(pl.multiple_of(tile + step * 16, 16), 16)
            real, imag = 0.0, 0.0
            for m in range(n + 1):
                kr, ki = spectrum[re, lanes[n - m]], spectrum[im, lanes[n - m]]
                sr, si = signal[re, lanes[m]], signal[im, lanes[m]]
                real = real + (kr * sr - ki * si)
                imag = imag + (kr * si + ki * sr)
            product[re, :] = real.astype(jnp.bfloat16)
            product[im, :] = imag.astype(jnp.bfloat16)

    def out_push(q):
        return pltpu.make_async_remote_copy(
            src_ref=outgoing.at[q], dst_ref=out.at[pl.ds(own_lane, own), :],
            send_sem=o_send.at[q], recv_sem=o_recv.at[i],
            device_id=(q, j), device_id_type=MESH_ID,
        )

    def out_keep(q):
        return pltpu.make_async_copy(
            outgoing.at[q], out.at[pl.ds(own_lane, own), :], o_send.at[q]
        )

    per_tile = tile // rows
    for n in range(blocks):
        lanes = slice(n * own, (n + 1) * own)
        for half in range(per_tile):
            project(n * per_tile + half, (2, 3), False, True)
            features(n * per_tile + half)
        signal[:, lanes] = jnp.dot(
            forward[:, tile:], wave[:, lanes], preferred_element_type=jnp.float32
        )
        multiply(n)
        smeared = jnp.dot(inverse[...], product[...], preferred_element_type=jnp.float32)
        for half in range(per_tile):
            q = n * per_tile + half
            at = slice(half * rows, (half + 1) * rows)
            mixed = smeared[at] + gain * wave[at, lanes].astype(jnp.float32)
            mixed = mixed.astype(jnp.bfloat16).astype(jnp.float32)
            gated = gate[q * rows : (q + 1) * rows, :] * mixed
            outgoing[q] = gated.T.astype(jnp.bfloat16)

            @pl.when(i != q)
            def _():
                out_push(q).start()

            @pl.when(i == q)
            def _():
                out_keep(q).start()

    for o in range(NZ):
        for h in halves:
            @pl.when(jnp.logical_and(o <= z, z < NZ - 1))
            def _():
                up(o, h).wait_send()

            @pl.when(jnp.logical_and(o >= z, z > 0))
            def _():
                down(o, h).wait_send()

            to_y(o, h).wait_send()
            for yy in range(NY):
                to_x(o, yy, h).wait_send()
        for yy in range(NY):
            for xx in range(NX):
                to_c(o, yy, xx).wait_send()
    for q in range(ctx_n):
        @pl.when(i != q)
        def _():
            weight_push(q).wait_send()
            out_push(q).wait_send()
            landed = out.at[pl.ds(q * own, own), :]
            pltpu.make_async_copy(landed, landed, o_recv.at[q]).wait()

        @pl.when(i == q)
        def _():
            out_keep(q).wait()


def fused_shards(tokens, in_weight, short_taps, long_filter, skip_gain):
    rows, depth = tokens.shape
    ctx_n, ch_n = NZ * NY, NX * NC
    own = long_filter.shape[1]
    span = rows * ctx_n
    tile = SPECTRAL
    lanes = span // tile * own
    forward, inverse = odd_frequency_tables(tile)
    vmem = pl.BlockSpec(memory_space=pltpu.VMEM)
    hbm = pl.BlockSpec(memory_space=pl.ANY)
    dma = pltpu.SemaphoreType.DMA
    flops = 2 * span * depth * ch_n * 3 * own
    return pl.pallas_call(
        mixer_kernel,
        out_shape=jax.ShapeDtypeStruct((ctx_n * own, rows), jnp.bfloat16),
        in_specs=[hbm, hbm, vmem, hbm, vmem, hbm, hbm],
        out_specs=hbm,
        scratch_shapes=[
            pltpu.VMEM(long_filter.shape, jnp.float32),
            pltpu.VMEM(forward.shape, jnp.bfloat16),
            pltpu.VMEM(inverse.shape, jnp.bfloat16),
            pltpu.VMEM((ctx_n * ch_n, rows, depth), jnp.bfloat16),
            pltpu.VMEM((ctx_n, in_weight.shape[1], 3 * own), jnp.bfloat16),
            pltpu.VMEM((depth * ch_n, 3 * own), jnp.bfloat16),
            pltpu.VMEM((8 + span, 3 * own), jnp.float32),
            pltpu.VMEM((2 * tile, lanes), jnp.float32),
            pltpu.VMEM((tile, lanes), jnp.bfloat16),
            pltpu.VMEM((2 * tile, lanes), jnp.float32),
            pltpu.VMEM((2 * tile, own), jnp.bfloat16),
            pltpu.VMEM((span, own), jnp.float32),
            pltpu.VMEM((ctx_n, own, rows), jnp.bfloat16),
            dma((6,)),
            dma((2 * ctx_n * ch_n,)),
            dma((4 * NZ,)),
            dma((2 * NZ,)),
            dma((2 * ctx_n,)),
            dma((ctx_n * NX,)),
            dma((ctx_n,)),
            dma((ctx_n,)),
            dma((ctx_n,)),
            dma((ctx_n,)),
        ],
        compiler_params=pltpu.CompilerParams(
            collective_id=0, has_side_effects=True, vmem_limit_bytes=56 * 1024 * 1024
        ),
        cost_estimate=pl.CostEstimate(
            flops=flops, bytes_accessed=2 * tokens.size * ctx_n * ch_n, transcendentals=0
        ),
        name="mixer",
    )(tokens, in_weight, short_taps, long_filter, skip_gain, jnp.asarray(forward), jnp.asarray(inverse))


def fits(mesh, tokens, in_weight, long_filter):
    span, depth = tokens.shape
    return (
        dict(mesh.shape) == {"ctx": NZ * NY, "ch": NX * NC}
        and span == NZ * NY * 256
        and depth == NX * NC * 1024
        and in_weight.shape[2] == long_filter.shape[0] * long_filter.shape[1]
        and long_filter.shape[1] == NZ * NY * 128
    )


def solution(mesh):
    placed = (
        P("ctx", "ch"),
        P(None, "ctx", "ch"),
        P(None, None, "ch"),
        P("ch", "ctx", None),
        P("ch", "ctx"),
    )

    def run(tokens, in_weight, short_taps, long_filter, skip_gain):
        body = fused_shards if fits(mesh, tokens, in_weight, long_filter) else shards
        return jax.shard_map(
            body, mesh=mesh, in_specs=placed, out_specs=P("ch", "ctx"), check_vma=False
        )(tokens, in_weight, short_taps, long_filter, skip_gain)

    return run
```
